256 devices in a mesh: grp: 4 (over x), kv: 64 (over y, z, core).
Axes of the slice: x: 4, y: 4, z: 8, core: 2. Of those that a mesh axis runs over, the one named last changes fastest.
Arguments:
- query_lat: bfloat16 [32, 128, 512], P('grp', 'kv'), may hold values from -122.91343 to 122.91343
- query_rope: bfloat16 [32, 128, 64], P('grp', 'kv'), may hold values from -6 to 6
- cache_lat: bfloat16 [32, 16384, 512], P('grp', 'kv'), may hold values from -6 to 6
- cache_rope: bfloat16 [32, 64, 16384], P('grp', None, 'kv'), may hold values from -6 to 6
- lengths: int32 [32], P('grp'), may hold values from 2048 to 16384, as said below
- w_value: bfloat16 [128, 512, 128], P('kv'), may hold values from -12 to 12
- w_out: bfloat16 [16384, 7168], P('kv'), may hold values from -0.125 to 0.125
- moe_tokens: bfloat16 [32, 7168], P('grp', 'kv'), may hold values from -6 to 6
- expert_ids: int32 [32, 8], P('grp'), may hold values from 0 to 31, all different within a row; in each aligned block of 8 rows (0 to 7, 8 to 15, ...) at most 4 rows name the same one
- route_weights: float32 [32, 8], P('grp'), may hold values from 0.1 to 1
- w_gate: bfloat16 [7168, 32768], P(None, ('grp', 'kv')), may hold values from -0.0625 to 0.0625
- w_up: bfloat16 [7168, 32768], P(None, ('grp', 'kv')), may hold values from -0.0625 to 0.0625
- w_down: bfloat16 [32768, 7168], P(('grp', 'kv')), may hold values from -0.75 to 0.75
Outputs:
- attn_out: bfloat16 [32, 7168], P('grp', 'kv')
- moe_out: bfloat16 [32, 7168], P('grp', 'kv')
The draws below stay inside these ranges and needn't reach their ends.
Inputs may be any that keep to these rules, and one draw needn't show every extreme that they name: `lengths`: in every group of 8 consecutive requests one has length 16384. `expert_ids`: each row names 8 different experts; among the 8 rows of one group no expert is named by more than 4 rows, and some expert of some group is named by exactly 4.
All inputs are finite; a program needn't handle non-finite values.
Results may differ from the reference program's by a relative error of at most 0.015.
Values may be sent and summed in bfloat16 or wider, within the bound.
No kernel may reach another device: no remote copies, remote signals or barrier semaphores. Data moves between devices by JAX's collectives and lax.ppermute only.
A program may use at most 64 MiB of HBM per device.

```python
import math
import jax
import jax.numpy as jnp
import numpy as np
from jax import lax

D = 7168
H = 128
LAT = 512
ROPE = 64
VH = 128
FF = 1024
R = 8
CTX_DEV = 256
CAP = 4
REQS = 32
CONTEXT = 16384
EXPERTS = 32
TOPK = 8
N_KV = 64


def anchor_rows(key):
    return jnp.clip(jax.random.normal(key, (REQS, 16, LAT), jnp.float32), -6.0, 6.0)


def draw_cache_lat(key, part):
    anchors = anchor_rows(key)
    key = jax.random.fold_in(key, 11)
    remainder = jnp.clip(jax.random.normal(key, (REQS, CONTEXT - 16, LAT), jnp.float32), -6.0, 6.0)
    return jnp.concatenate([anchors, remainder], axis=1).astype(jnp.bfloat16)


def draw_query_lat(key, part):
    key = jax.random.fold_in(key, 12)
    subkeys = jax.random.split(key, 1)
    drawn_query = jnp.clip(jax.random.normal(subkeys[0], (REQS, H, LAT), jnp.float32), -6.0, 6.0)
    return drawn_query.astype(jnp.bfloat16)


def draw_lengths(key, part):
    key = jax.random.fold_in(key, 14)
    subkeys = jax.random.split(key, 2)
    drawn_len = jax.random.randint(subkeys[0], (REQS,), CONTEXT // 8, CONTEXT + 1)
    full_slot = jax.random.randint(subkeys[1], (REQS // R,), 0, R)
    request = lax.iota(jnp.int32, REQS)
    is_full = request % R == full_slot[request // R]
    return jnp.where(is_full, CONTEXT, drawn_len).astype(jnp.int32)


def spiked(drawn, stream_key, source, target, parts, factor):
    def block_of(dim):
        return (jnp.arange(drawn.shape[dim]) // (drawn.shape[dim] // parts)).reshape((-1,) + (1,) * (drawn.ndim - 1 - dim))

    first = jax.random.permutation(stream_key, parts)[block_of(target)]
    other_side = (block_of(target) + parts // 2) % parts
    return jnp.where((block_of(source) == first) | (block_of(source) == other_side), factor * drawn, drawn)


def steps_of(stream_key, extent, pieces, least, largest):
    factor_of, own = 1.0, jax.random.fold_in(stream_key, 6)
    for axis_at, shards_of in pieces:
        draws = jnp.exp(jax.random.uniform(jax.random.fold_in(own, axis_at), (shards_of,), jnp.float32, least / len(pieces), largest / len(pieces)))
        factor_of = factor_of * jnp.repeat(draws, extent[axis_at] // shards_of).reshape([-1 if axis == axis_at else 1 for axis in range(len(extent))])
    return factor_of


def routed_block(own_key, own, number, rows, amount, top, limit, slope):
    sequence = jax.random.permutation(own_key, amount)
    packed, common = load_shares(amount, rows * top, limit, slope, True), load_shares(amount, rows * top, limit, slope, False)
    places = jnp.arange(amount)

    def named(sizes, turn):
        used = int((sizes > 0).sum())
        fixed = max(1, used // 4)
        passed = fixed + (places - fixed + turn * (used - fixed)) % max(1, amount - fixed)
        return jnp.zeros((amount,), jnp.int32).at[sequence[jnp.where(places < fixed, places, passed)]].set(jnp.asarray(sizes, jnp.int32))

    sizes = jnp.where(number % 4 == 0, named(packed, number // 4), named(common, number - number // 4 - 1))
    mixed = jax.random.permutation(jax.random.fold_in(own, 3), amount)
    donor, sink = mixed[0:amount // 2 * 2:2], mixed[1:amount // 2 * 2:2]
    slack = jnp.minimum(sizes[donor] - 1, limit - sizes[sink]) // 2
    slack = jnp.where((donor == sequence[0]) | (sink == sequence[0]) | (sizes[sink] == 0), 0, jnp.maximum(slack, 0))
    passed = jax.random.randint(jax.random.fold_in(own, 4), (amount // 2,), 0, 1 << 20) % (slack + 1)
    sizes = sizes.at[donor].add(-passed).at[sink].add(passed)
    items = jnp.searchsorted(jnp.cumsum(sizes), jnp.arange(rows * top), side="right").astype(jnp.int32)
    listing = items.reshape(top, rows).T
    listing = listing[jax.random.permutation(jax.random.fold_in(own, 1), rows)]
    turn = jax.random.randint(jax.random.fold_in(own, 2), (rows, 1), 0, top)
    return jnp.take_along_axis(listing, (jnp.arange(top)[None, :] + turn) % top, axis=1)


def load_shares(amount, total, most, slope, full):
    loads = [(1 << 20) // math.isqrt(grade ** slope) + 1 for grade in range(1, amount + 1)]
    largest = most if full else min(most, max(-(-total // amount), total * loads[0] // sum(loads)))
    least = 1 if total - largest >= amount - 1 else 0
    given, rest = [largest] + [least] * (amount - 1), total - largest - least * (amount - 1)
    while rest > 0:
        candidates = [i for i in range(1, amount) if given[i] < largest] or [i for i in range(1, amount) if given[i] < most]
        whole, remaining = sum([loads[i] for i in candidates]), rest
        for i in candidates:
            extra = min(most - given[i], max(1, remaining * loads[i] // whole), rest)
            given[i] = given[i] + extra
            rest = rest - extra
    return np.array(given)


def centred(rng, extent, deviation, reach, shards=(), dtype=jnp.bfloat16):
    drawn = jax.random.normal(rng, extent, jnp.float32) * deviation
    if len(shards) > 0:
        drawn = steps_of(rng, extent, shards, -0.22, 0.18) * drawn
    return jnp.clip(drawn, min=-reach, max=reach).astype(dtype)


def bell_draw_with(key, dims, spread, limit, shards, heavy, dtype=jnp.bfloat16):
    drawn = spread * jax.random.normal(key, dims, jnp.float32)
    if shards:
        drawn = drawn * steps_of(key, dims, shards, -0.22, 0.18)
    return jnp.clip(spiked(drawn, jax.random.fold_in(key, 3), *heavy), -limit, limit).astype(dtype)


def setup_inputs(seed: int = 0) -> dict:
    splits = jax.random.split(jax.random.key(seed), 14)
    query_lat = draw_query_lat(jax.random.fold_in(splits[13], 71), 0)
    query_rope = centred(splits[1], (REQS, H, ROPE), 1.0, 6.0, ((0, 4), (1, 64)))
    cache_lat = draw_cache_lat(jax.random.fold_in(splits[13], 71), 0)
    cache_rope = centred(splits[3], (REQS, ROPE, CONTEXT), 1.0, 6.0, ((0, 4), (2, 64)))
    lengths = draw_lengths(jax.random.fold_in(splits[13], 71), 0)
    w_value = centred(splits[5], (H, LAT, VH), 2.0, 12.0, ((0, 64),))
    w_out = bell_draw_with(splits[6], (H * VH, D), (H * VH) ** -0.5, 0.125, ((0, 64),), (0, 1, 64, 4.0))
    moe_tokens = centred(splits[7], (REQS, D), 1.0, 6.0, ((0, 4), (1, 64)))
    expert_ids_keys = jax.random.split(jax.random.fold_in(splits[8], 1), REQS // R)
    expert_ids_turns = jax.random.permutation(jax.random.fold_in(splits[8], 3), REQS // R)
    expert_ids = jax.vmap(lambda own, number: routed_block(jax.random.fold_in(splits[8], 2), own, number, R, EXPERTS, TOPK, CAP, 2))(expert_ids_keys, expert_ids_turns).reshape((REQS, TOPK))
    route_weights = jnp.clip(0.1 + 0.9 * jax.random.uniform(splits[9], (REQS, TOPK), jnp.float32) ** steps_of(splits[9], (REQS, TOPK), ((0, 4),), -0.2, 0.2), 0.1, 1.0)
    w_gate = centred(splits[10], (D, EXPERTS * FF), D ** -0.5, 0.0625, ((1, 256),))
    w_up = centred(splits[11], (D, EXPERTS * FF), D ** -0.5, 0.0625, ((1, 256),))
    w_down = bell_draw_with(splits[12], (EXPERTS * FF, D), FF ** -0.5, 0.75, ((0, 256),), (0, 1, 256, 6.0))
    return dict(query_lat=query_lat, query_rope=query_rope, cache_lat=cache_lat, cache_rope=cache_rope, lengths=lengths, w_value=w_value, w_out=w_out, moe_tokens=moe_tokens, expert_ids=expert_ids, route_weights=route_weights, w_gate=w_gate, w_up=w_up, w_down=w_down)


def attend_request(operands):
    query_lat, query_rope, cache_lat, cache_rope, length = operands
    score_scale = (VH + ROPE) ** -0.5
    scores = (jnp.dot(query_lat, cache_lat.T, preferred_element_type=jnp.float32)
              + jnp.dot(query_rope, cache_rope, preferred_element_type=jnp.float32)) * score_scale
    usable = lax.iota(jnp.int32, CONTEXT)[None, :] < length.astype(jnp.int32)
    scores = jnp.where(usable, scores, -1e30).reshape(H, N_KV, CTX_DEV)
    usable_blocks = usable.reshape(1, N_KV, CTX_DEV)
    block_max = jnp.max(scores, axis=2)
    weights = jnp.where(usable_blocks, jnp.exp(scores - block_max[:, :, None]), 0.0)
    block_tot = jnp.sum(weights, axis=2)
    weights_half = lax.optimization_barrier(weights.astype(jnp.bfloat16))
    weighted = jnp.einsum("hbt,btl->hbl", weights_half.astype(jnp.float32),
                          cache_lat.reshape(N_KV, CTX_DEV, LAT).astype(jnp.float32))
    partial_value = (weighted / jnp.maximum(block_tot, 1.0)[:, :, None]).astype(jnp.bfloat16)
    partial_value = lax.optimization_barrier(partial_value)
    peak = jnp.max(block_max, axis=1, keepdims=True)
    scale_b = block_tot * jnp.exp(block_max - peak)
    numerator = jnp.sum(partial_value.astype(jnp.float32) * scale_b[:, :, None], axis=1)
    denominator = jnp.sum(scale_b, axis=1)
    return (numerator / denominator[:, None]).astype(jnp.bfloat16)


def reference(query_lat, query_rope, cache_lat, cache_rope, lengths, w_value, w_out,
              moe_tokens, expert_ids, route_weights, w_gate, w_up, w_down):
    latent_half = lax.map(attend_request, (query_lat, query_rope, cache_lat, cache_rope, lengths))
    head_values = jnp.einsum("rhl,hlv->rhv", latent_half.astype(jnp.float32),
                             w_value.astype(jnp.float32)).astype(jnp.bfloat16)
    attn_out = jnp.dot(head_values.reshape(REQS, H * VH), w_out,
                       preferred_element_type=jnp.float32).astype(jnp.bfloat16)

    picked = expert_ids[:, :, None] == lax.iota(jnp.int32, EXPERTS)[None, None, :]
    coefficient = jnp.sum(jnp.where(picked, route_weights[:, :, None], 0.0), axis=1)

    def add_expert(running, expert):
        offset = (expert * FF).astype(jnp.int32)
        gate_proj = jnp.dot(moe_tokens, lax.dynamic_slice_in_dim(w_gate, offset, FF, 1),
                            preferred_element_type=jnp.float32)
        up_proj = jnp.dot(moe_tokens, lax.dynamic_slice_in_dim(w_up, offset, FF, 1),
                          preferred_element_type=jnp.float32)
        hidden = (jax.nn.silu(gate_proj) * up_proj).astype(jnp.bfloat16)
        expert_out = jnp.dot(hidden, lax.dynamic_slice_in_dim(w_down, offset, FF, 0),
                             preferred_element_type=jnp.float32)
        column = lax.dynamic_slice_in_dim(coefficient, expert.astype(jnp.int32), 1, 1)
        return running + column * expert_out, None

    running = jnp.zeros((REQS, D), jnp.float32)
    running, unused_out = lax.scan(add_expert, running, lax.iota(jnp.int32, EXPERTS))
    return attn_out, running.astype(jnp.bfloat16)
```

```python
import jax
import jax.numpy as jnp
from jax import lax
from jax.experimental import pallas as pl
from jax.experimental.pallas import tpu as pltpu
from jax.sharding import Mesh
from jax.sharding import PartitionSpec as P

FF = 1024
F32 = jnp.float32
BF16 = jnp.bfloat16
LANES = 128


def three_terms(value):
    high = value.astype(BF16).astype(F32)
    rest = value - high
    middle = rest.astype(BF16).astype(F32)
    return high, middle, rest - middle


def attention_kernel(
    info, query, lat_own, lat_far, rope_own, rope_far, out, query_rows, out_rows, *, scale
):
    request = pl.program_id(0)
    peers, chunk, width = query.shape
    latent = lat_own.shape[2]
    rope = rope_own.shape[1]
    requests = pl.num_programs(0)
    rows = peers * chunk // 8

    @pl.when(request == 0)
    def _():
        for tile in range(width // LANES):
            piece = query[:, :, tile * LANES : (tile + 1) * LANES].astype(F32)
            query_rows[tile] = piece.reshape(peers * chunk, LANES)

    mine = jnp.concatenate(
        [query_rows[tile, pl.ds(request, rows, stride=8), :] for tile in range(width // LANES)],
        axis=1,
    ).astype(BF16)
    length = info[request]
    parts = []
    for lat, rot, base in (
        (lat_own, rope_own, info[requests]),
        (lat_far, rope_far, info[requests + 1]),
    ):
        score = (
            lax.dot_general(
                mine[:, :latent],
                lat[0],
                (((1,), (1,)), ((), ())),
                preferred_element_type=F32,
            )
            + jnp.dot(mine[:, latent : latent + rope], rot[0], preferred_element_type=F32)
        ) * scale
        usable = base + lax.broadcasted_iota(jnp.int32, score.shape, 1) < length
        parts.append((jnp.where(usable, score, -1e30), usable, lat))
    top = jnp.maximum(
        jnp.max(parts[0][0], axis=1, keepdims=True), jnp.max(parts[1][0], axis=1, keepdims=True)
    )
    total = jnp.zeros_like(top)
    weighted = jnp.zeros((rows, latent), F32)
    for score, usable, lat in parts:
        weight = jnp.where(usable, jnp.exp(score - top), 0.0)
        total += jnp.sum(weight, axis=1, keepdims=True)
        weighted += jnp.dot(weight.astype(BF16), lat[0], preferred_element_type=F32)
    partial = weighted / jnp.maximum(total, 1.0)
    lane = lax.broadcasted_iota(jnp.int32, (rows, LANES), 1)
    stats = jnp.zeros((rows, LANES), F32)
    for place, term in enumerate(three_terms(top) + three_terms(total)):
        stats = jnp.where(lane == place, term, stats)
    tiles = latent // LANES
    for tile in range(tiles):
        out_rows[tile, pl.ds(request, rows, stride=8), :] = partial[
            :, tile * LANES : (tile + 1) * LANES
        ]
    out_rows[tiles, pl.ds(request, rows, stride=8), :] = stats

    @pl.when(request == requests - 1)
    def _():
        for tile in range(tiles + 1):
            out[:, tile * chunk : (tile + 1) * chunk, :] = (
                out_rows[tile].reshape(peers, chunk, LANES).astype(BF16)
            )


def attention(info, query, lat_own, lat_far, rope_own, rope_far, scale):
    peers, chunk, width = query.shape
    requests, positions, latent = lat_own.shape
    rope = rope_own.shape[1]
    lat_spec = pl.BlockSpec((1, positions, latent), lambda r: (r, 0, 0))
    rope_spec = pl.BlockSpec((1, rope, positions), lambda r: (r, 0, 0))
    out_shape = (peers, (latent // LANES + 1) * chunk, LANES)
    return pl.pallas_call(
        lambda *refs: attention_kernel(*refs, scale=scale),
        out_shape=jax.ShapeDtypeStruct(out_shape, BF16),
        grid=(requests,),
        in_specs=[
            pl.BlockSpec(memory_space=pltpu.SMEM),
            pl.BlockSpec((peers, chunk, width), lambda r: (0, 0, 0)),
            lat_spec,
            lat_spec,
            rope_spec,
            rope_spec,
        ],
        out_specs=pl.BlockSpec(out_shape, lambda r: (0, 0, 0)),
        scratch_shapes=[
            pltpu.VMEM((width // LANES, peers * chunk, LANES), F32),
            pltpu.VMEM((latent // LANES + 1, peers * chunk, LANES), F32),
        ],
        compiler_params=pltpu.CompilerParams(vmem_limit_bytes=20 * 2**20),
        cost_estimate=pl.CostEstimate(
            flops=2 * peers * chunk * 2 * positions * (2 * latent + rope),
            bytes_accessed=6 * 2**20,
            transcendentals=peers * chunk * 2 * positions,
        ),
        name="attention",
    )(info, query, lat_own, lat_far, rope_own, rope_far)


def experts_kernel(own, one, two, three, swapped, weight, gate, up, down, out, rows_ref):
    peers, chunk, _ = own.shape
    span = gate.shape[0] // (2 * peers)
    half = span // 2
    first = LANES - 64
    core = weight[0:1, LANES - 1 :] > 0.0
    near = (own, one, two, three)
    for peer in range(peers):
        for block in range(4):
            mine = near[block][peer].astype(F32)
            theirs = swapped[block, peer].astype(F32)
            pieces = []
            for side in (mine, theirs):
                pieces.append(
                    jnp.concatenate(
                        [side[:8, first : first + half], side[8:, first : first + half]], axis=1
                    )
                )
            even = jnp.where(core, pieces[1], pieces[0])
            odd = jnp.where(core, pieces[0], pieces[1])
            begin = 2 * peer * span
            rows_ref[8 * block : 8 * block + 8, begin : begin + 2 * span] = jnp.concatenate(
                [even, odd], axis=1
            )
    tokens = rows_ref[...].astype(BF16)
    gate_proj = jnp.dot(tokens, gate[...], preferred_element_type=F32)
    up_proj = jnp.dot(tokens, up[...], preferred_element_type=F32)
    hidden = (gate_proj * jax.nn.sigmoid(gate_proj) * up_proj).astype(BF16)
    share = weight[:, 0:1]
    width = down.shape[1]
    step = 1024
    for start in range(0, width, step):
        result = jnp.dot(hidden, down[:, start : start + step], preferred_element_type=F32) * share
        for block in range(4):
            out[block, :, start : start + step] = result[8 * block : 8 * block + 8].astype(BF16)


def experts(near, swapped, weight, gate, up, down):
    depth, units = gate.shape
    width = down.shape[1]
    return pl.pallas_call(
        experts_kernel,
        out_shape=jax.ShapeDtypeStruct((4, 8, width), BF16),
        in_specs=[pl.BlockSpec(memory_space=pltpu.VMEM)] * 9,
        out_specs=pl.BlockSpec(memory_space=pltpu.VMEM),
        scratch_shapes=[pltpu.VMEM((32, depth), F32)],
        compiler_params=pltpu.CompilerParams(vmem_limit_bytes=20 * 2**20),
        cost_estimate=pl.CostEstimate(
            flops=2 * 32 * 3 * depth * units, bytes_accessed=8 * 2**20, transcendentals=0
        ),
        name="experts",
    )(*near, swapped, weight, gate, up, down)


def merge_kernel(got, value, project, moe_own, moe_one, moe_two, moe_three, out):
    peers, height, _ = got.shape
    chunk = 16
    tiles = height // chunk - 1
    stats = got[:, tiles * chunk :, :].astype(F32)
    top = stats[:, :, 0:1] + stats[:, :, 1:2] + stats[:, :, 2:3]
    total = stats[:, :, 3:4] + stats[:, :, 4:5] + stats[:, :, 5:6]
    peak = jnp.max(top, axis=0, keepdims=True)
    share = total * jnp.exp(top - peak)
    denominator = jnp.sum(share, axis=0)
    columns = []
    for tile in range(tiles):
        piece = got[:, tile * chunk : (tile + 1) * chunk, :].astype(F32)
        columns.append(jnp.sum(piece * share, axis=0) / denominator)
    merged = jnp.concatenate(columns, axis=1)
    heads = []
    for head in range(2):
        rows = merged[8 * head : 8 * head + 8].astype(BF16)
        heads.append(jnp.dot(rows, value[head], preferred_element_type=F32))
    head_values = jnp.concatenate(heads, axis=1).astype(BF16)
    attended = jnp.dot(head_values, project[...], preferred_element_type=F32)
    routed = (
        moe_own[...].astype(F32)
        + moe_one[...].astype(F32)
        + moe_two[...].astype(F32)
        + moe_three[...].astype(F32)
    )
    both = jnp.concatenate([attended, routed], axis=0)
    count, _, span = out.shape
    for place in range(count):
        out[place] = both[:, place * span : (place + 1) * span].astype(BF16)


def merge(got, value, project, moe, count):
    width = project.shape[1]
    return pl.pallas_call(
        merge_kernel,
        out_shape=jax.ShapeDtypeStruct((count, 16, width // count), BF16),
        in_specs=[pl.BlockSpec(memory_space=pltpu.VMEM)] * 7,
        out_specs=pl.BlockSpec(memory_space=pltpu.VMEM),
        compiler_params=pltpu.CompilerParams(vmem_limit_bytes=20 * 2**20),
        cost_estimate=pl.CostEstimate(
            flops=2 * 8 * project.shape[0] * width, bytes_accessed=6 * 2**20, transcendentals=0
        ),
        name="merge",
    )(got, value, project, *moe)


def shards(
    query_lat,
    query_rope,
    cache_lat,
    cache_rope,
    lengths,
    w_value,
    w_out,
    moe_tokens,
    expert_ids,
    route_weights,
    w_gate,
    w_up,
    w_down,
):
    plane = ("y", "z")
    kv = ("y", "z", "c")
    shard_count = lax.axis_size(kv)
    shard_index = lax.axis_index(kv)
    core = lax.axis_index("c")
    group_count = lax.axis_size("x")
    peers = lax.axis_size(plane)
    requests, positions, latent = cache_lat.shape
    head_share = query_lat.shape[1]
    rope = query_rope.shape[2]
    span = moe_tokens.shape[1]
    swap = [(0, 1), (1, 0)]

    def along_x(value, shift):
        return lax.ppermute(
            value, "x", [(i, (i + shift) % group_count) for i in range(group_count)]
        )

    halves = moe_tokens.reshape(requests, head_share, span // head_share)
    spare = -(latent + rope + span // head_share) % LANES
    payload = jnp.concatenate(
        [query_lat, query_rope, halves, jnp.zeros((requests, head_share, spare), BF16)], axis=2
    )
    payload = payload.transpose(1, 0, 2).reshape(1, head_share * requests, -1)
    payload = jnp.broadcast_to(payload, (peers,) + payload.shape[1:])
    query = lax.all_to_all(payload, plane, 0, 0, tiled=True)
    lat_far = lax.ppermute(cache_lat, "c", swap)
    rope_far = lax.ppermute(cache_rope, "c", swap)

    expert_count = group_count * shard_count * w_gate.shape[1] // FF
    numbers = lax.iota(jnp.int32, expert_count)
    picked = expert_ids[:, :, None] == numbers[None, None, :]
    coefficient = jnp.sum(jnp.where(picked, route_weights[:, :, None], 0.0), axis=1)
    coefficients = [coefficient] + [along_x(coefficient, d) for d in range(1, group_count)]
    here = (lax.axis_index("x") * shard_count + shard_index) * w_gate.shape[1] // FF
    weight = jnp.sum(
        jnp.where(numbers == here, jnp.concatenate(coefficients, axis=0), 0.0),
        axis=1,
        keepdims=True,
    )
    weight = jnp.broadcast_to(weight, (group_count * requests, LANES))
    weight = jnp.where(lax.iota(jnp.int32, LANES) == LANES - 1, core.astype(F32), weight)

    info = jnp.concatenate(
        [lengths, jnp.stack([shard_index * positions, (shard_index + 1 - 2 * core) * positions])]
    )
    scale = (w_value.shape[2] + rope) ** (-0.5)
    raw = query[:, :, latent:]
    near = [raw] + [along_x(raw, d) for d in range(1, group_count)]
    part = attention(info, query, cache_lat, lat_far, cache_rope, rope_far, scale)
    got = lax.all_to_all(part, plane, 0, 0, tiled=True)

    swapped = lax.ppermute(jnp.stack(near), "c", swap)
    routed = experts(near, swapped, weight, w_gate, w_up, w_down)
    moe = [routed[0]] + [along_x(routed[d], -d) for d in range(1, group_count)]

    terms = merge(got, w_value, w_out, moe, shard_count)
    arrived = lax.all_to_all(terms, kv, 0, 0, tiled=True)
    summed = jnp.sum(arrived.astype(F32), axis=0).astype(BF16)
    return (summed[:requests], summed[requests:])


def solution(mesh):
    groups = mesh.shape["grp"]
    split = Mesh(mesh.devices.reshape(groups, 4, 8, 2), ("x", "y", "z", "c"))
    kv = ("y", "z", "c")
    both = ("x",) + kv
    return jax.shard_map(
        shards,
        mesh=split,
        in_specs=(
            P("x", kv, None),
            P("x", kv, None),
            P("x", kv, None),
            P("x", None, kv),
            P("x"),
            P(kv, None, None),
            P(kv, None),
            P("x", kv),
            P("x", None),
            P("x", None),
            P(None, both),
            P(None, both),
            P(both, None),
        ),
        out_specs=(P("x", kv), P("x", kv)),
        check_vma=False,
    )
```

```python
import jax
import jax.numpy as jnp
from jax import lax
from jax.experimental import pallas as pl
from jax.experimental.pallas import tpu as pltpu
from jax.sharding import Mesh
from jax.sharding import PartitionSpec as P

FF = 1024
CAP = 4
ROWS = 8
F32 = jnp.float32
BF16 = jnp.bfloat16
LANES = 128
KV = ("y", "z", "c")
VMEM = pl.BlockSpec(memory_space=pltpu.VMEM)
SMEM = pl.BlockSpec(memory_space=pltpu.SMEM)
HBM = pl.BlockSpec(memory_space=pltpu.HBM)


def three_terms(value):
    high = value.astype(BF16).astype(F32)
    rest = value - high
    middle = rest.astype(BF16).astype(F32)
    return high, middle, rest - middle


def params(mebibytes):
    return pltpu.CompilerParams(vmem_limit_bytes=mebibytes * 2**20)


def payload_kernel(query_lat, query_rope, tokens, out):
    peers = out.shape[0]
    latent, rope = query_lat.shape[2], query_rope.shape[2]
    heads = query_lat.shape[1]
    half = tokens.shape[1] // heads
    lat = query_lat[...].astype(F32)
    rot = query_rope[...].astype(F32)
    tok = tokens[...].astype(F32)
    spare = jnp.zeros((ROWS, out.shape[2] - latent - rope - half), F32)
    rows = []
    for head in range(heads):
        tail = jnp.concatenate(
            [rot[:, head, :], tok[:, head * half : (head + 1) * half], spare], axis=1
        )
        rows.append(jnp.concatenate([lat[:, head, :], tail], axis=1))
    chunk = jnp.concatenate(rows, axis=0).astype(BF16)
    for peer in range(peers):
        out[peer] = chunk


def payload(query_lat, query_rope, tokens, peers):
    requests, heads, latent = query_lat.shape
    return pl.pallas_call(
        payload_kernel,
        out_shape=jax.ShapeDtypeStruct((peers, heads * requests, latent + LANES), BF16),
        in_specs=[VMEM] * 3,
        out_specs=VMEM,
        compiler_params=params(20),
        name="payload",
    )(query_lat, query_rope, tokens)


def attention_kernel(
    lengths,
    query,
    lat_own,
    lat_far,
    rope_own,
    rope_far,
    ids,
    route,
    out,
    send_0,
    send_1,
    send_2,
    send_3,
    mix_out,
    query_rows,
    out_rows,
    stat_rows,
    token_rows,
    *,
    scale,
    units,
):
    peers, chunk, width = query.shape
    requests, positions, latent = lat_own.shape
    rope = rope_own.shape[1]
    tiles = latent // LANES
    heads = chunk // requests
    group, groups = lax.axis_index("x"), lax.axis_size("x")
    shard, shards_here = lax.axis_index(KV), lax.axis_size(KV)
    core = lax.axis_index("c")
    rows = peers * heads

    for tile in range(tiles + 1):
        piece = query[:, :, tile * LANES : (tile + 1) * LANES].astype(F32)
        query_rows[tile] = piece.reshape(peers * chunk, LANES)

    lane = lax.broadcasted_iota(jnp.int32, (rows, LANES), 1)
    stats = jnp.zeros((rows, LANES), F32)
    base_own = shard * positions
    base_far = (shard + 1 - 2 * core) * positions
    place = lax.broadcasted_iota(jnp.int32, (rows, positions), 1)
    for request in range(requests):
        mine = jnp.concatenate(
            [
                jnp.concatenate(
                    [
                        query_rows[tile, pl.ds(requests * head + request, peers, stride=chunk), :]
                        for tile in range(tiles + 1)
                    ],
                    axis=1,
                )
                for head in range(heads)
            ],
            axis=0,
        ).astype(BF16)
        length = lengths[request]
        parts = []
        for lat, rot, base in ((lat_own, rope_own, base_own), (lat_far, rope_far, base_far)):
            score = (
                lax.dot_general(
                    mine[:, :latent],
                    lat[request],
                    (((1,), (1,)), ((), ())),
                    preferred_element_type=F32,
                )
                + jnp.dot(
                    mine[:, latent : latent + rope], rot[request], preferred_element_type=F32
                )
            ) * scale
            usable = place < length - base
            parts.append((jnp.where(usable, score, -1e30), usable, lat))
        top = jnp.max(jnp.maximum(parts[0][0], parts[1][0]), axis=1, keepdims=True)
        weights = [jnp.where(usable, jnp.exp(score - top), 0.0) for score, usable, _ in parts]
        total = jnp.sum(weights[0] + weights[1], axis=1, keepdims=True)
        weighted = jnp.dot(
            weights[0].astype(BF16), lat_own[request], preferred_element_type=F32
        ) + jnp.dot(weights[1].astype(BF16), lat_far[request], preferred_element_type=F32)
        partial = weighted / jnp.maximum(total, 1.0)
        for index, term in enumerate(three_terms(top) + three_terms(total)):
            stats = jnp.where(lane == ROWS * request + index, term, stats)
        for head in range(heads):
            for tile in range(tiles):
                out_rows[tile, pl.ds(requests * head + request, peers, stride=chunk), :] = partial[
                    peers * head : peers * (head + 1), tile * LANES : (tile + 1) * LANES
                ]

    for tile in range(tiles):
        out[:, tile * chunk : (tile + 1) * chunk, :] = (
            out_rows[tile].reshape(peers, chunk, LANES).astype(BF16)
        )
    stat_rows[...] = jnp.zeros_like(stat_rows)
    for head in range(heads):
        stat_rows[pl.ds(head, peers, stride=ROWS), :] = stats[peers * head : peers * (head + 1)]
    out[:, tiles * chunk :, :] = stat_rows[...].reshape(peers, ROWS, LANES).astype(BF16)

    half = token_rows.shape[1] // (peers * heads)
    for peer in range(peers):
        begin = peer * chunk
        pieces = [
            query_rows[tiles, begin + requests * head : begin + requests * (head + 1), :][
                :, rope : rope + half
            ]
            for head in range(heads)
        ]
        token_rows[:, peer * heads * half : (peer + 1) * heads * half] = jnp.concatenate(
            pieces, axis=1
        )
    tokens = token_rows[...].astype(BF16)
    named = ids[...]
    strength = route[...]
    lower = (
        lax.broadcasted_iota(jnp.int32, (ROWS, ROWS), 1)
        < lax.broadcasted_iota(jnp.int32, (ROWS, ROWS), 0)
    ).astype(F32)
    slot_lane = lax.broadcasted_iota(jnp.int32, (ROWS, LANES), 1)
    placing = jnp.zeros((ROWS, LANES), F32)
    mix = jnp.zeros((ROWS, LANES), F32)
    for step in range(4):
        expert = (lax.rem(group + step, groups) * shards_here + shard) * units // FF
        hit = named == expert
        chosen = jnp.max(jnp.where(hit, 1.0, 0.0), axis=1, keepdims=True)
        weight = jnp.sum(jnp.where(hit, strength, 0.0), axis=1, keepdims=True)
        chosen_wide = jnp.broadcast_to(chosen, (ROWS, LANES))
        rank = jnp.dot(lower, chosen_wide, preferred_element_type=F32)
        picked = (rank == (slot_lane - CAP * step).astype(F32)) & (chosen_wide > 0.0)
        picked = picked & (slot_lane >= CAP * step) & (slot_lane < CAP * (step + 1))
        placing = jnp.where(picked, 1.0, placing)
        mix = jnp.where(picked, weight, mix)
    mix_out[...] = mix
    select = placing.T[: 4 * CAP, :].astype(BF16)
    chosen_rows = jnp.dot(select, tokens, preferred_element_type=F32).astype(BF16)
    for step, send in enumerate((send_0, send_1, send_2, send_3)):
        send[...] = chosen_rows[CAP * step : CAP * (step + 1)]


def attention(lengths, query, lat_own, lat_far, rope_own, rope_far, ids, route, scale, span, units):
    peers, chunk, width = query.shape
    requests, positions, latent = lat_own.shape
    rope = rope_own.shape[1]
    tiles = latent // LANES
    return pl.pallas_call(
        lambda *refs: attention_kernel(*refs, scale=scale, units=units),
        out_shape=[jax.ShapeDtypeStruct((peers, tiles * chunk + ROWS, LANES), BF16)]
        + [jax.ShapeDtypeStruct((CAP, peers * span), BF16)] * 4
        + [jax.ShapeDtypeStruct((ROWS, LANES), F32)],
        in_specs=[SMEM] + [VMEM] * 7,
        out_specs=[VMEM] * 6,
        scratch_shapes=[
            pltpu.VMEM((width // LANES, peers * chunk, LANES), F32),
            pltpu.VMEM((tiles, peers * chunk, LANES), F32),
            pltpu.VMEM((peers * ROWS, LANES), F32),
            pltpu.VMEM((requests, peers * span), F32),
        ],
        compiler_params=params(24),
        cost_estimate=pl.CostEstimate(
            flops=2 * peers * chunk * 2 * positions * (2 * latent + rope),
            bytes_accessed=6 * 2**20,
            transcendentals=peers * chunk * 2 * positions,
        ),
        name="attention",
    )(lengths, query, lat_own, lat_far, rope_own, rope_far, ids, route)


def experts_kernel(
    own, far, gate, up, down, out_0, out_1, out_2, out_3, gate_in, up_in, down_in, sems
):
    depth = gate.shape[0]
    span = 112
    blocks = depth // (2 * span)
    pieces = 4
    piece = depth // pieces
    core = lax.axis_index("c")
    copies = []
    for index in range(pieces):
        rows = pl.ds(index * piece, piece)
        for number, (source, target) in enumerate(((gate, gate_in), (up, up_in))):
            copies.append(
                pltpu.make_async_copy(
                    source.at[rows, :], target.at[rows, :], sems.at[2 * index + number]
                )
            )
    last = pltpu.make_async_copy(down, down_in, sems.at[2 * pieces])
    for copy in copies:
        copy.start()
    last.start()
    total = jnp.zeros((own.shape[0], 2 * gate.shape[1]), F32)
    each = blocks // pieces
    for index in range(pieces):
        copies[2 * index].wait()
        copies[2 * index + 1].wait()
        for tokens, parity in ((own, core), (far, 1 - core)):
            columns = []
            for source in (gate_in, up_in):
                columns.append(
                    jnp.concatenate(
                        [
                            source[
                                pl.ds(
                                    pl.multiple_of(2 * span * block + span * parity, 16), span
                                ),
                                :,
                            ]
                            for block in range(each * index, each * (index + 1))
                        ],
                        axis=0,
                    )
                )
            total += jnp.dot(
                tokens[:, each * span * index : each * span * (index + 1)],
                jnp.concatenate(columns, axis=1),
                preferred_element_type=F32,
            )
    units = gate.shape[1]
    gate_proj, up_proj = total[:, :units], total[:, units:]
    hidden = (gate_proj * jax.nn.sigmoid(gate_proj) * up_proj).astype(BF16)
    last.wait()
    width = down.shape[1]
    step = 1024
    for start in range(0, width, step):
        result = jnp.dot(hidden, down_in[:, start : start + step], preferred_element_type=F32)
        result = result.astype(BF16)
        for block, out in enumerate((out_0, out_1, out_2, out_3)):
            out[:, start : start + step] = result[CAP * block : CAP * (block + 1)]


def experts(own, far, gate, up, down):
    depth, units = gate.shape
    width = down.shape[1]
    return pl.pallas_call(
        experts_kernel,
        out_shape=[jax.ShapeDtypeStruct((CAP, width), BF16)] * 4,
        in_specs=[VMEM] * 2 + [HBM] * 3,
        out_specs=[VMEM] * 4,
        scratch_shapes=[
            pltpu.VMEM((depth, units), BF16),
            pltpu.VMEM((depth, units), BF16),
            pltpu.VMEM((units, width), BF16),
            pltpu.SemaphoreType.DMA((9,)),
        ],
        compiler_params=params(24),
        cost_estimate=pl.CostEstimate(
            flops=2 * 16 * 3 * depth * units, bytes_accessed=6 * 2**20, transcendentals=0
        ),
        name="experts",
    )(own, far, gate, up, down)


def merge_kernel(
    got, value, project, mix, back_0, back_1, back_2, back_3, keep, send, project_in, sem
):
    copy = pltpu.make_async_copy(project, project_in, sem)
    copy.start()
    peers, height, _ = got.shape
    heads = value.shape[0]
    chunk = ROWS * heads
    tiles = height // chunk
    core = lax.axis_index("c")
    stats = got[:, tiles * chunk :, :].astype(F32)
    lane = lax.broadcasted_iota(jnp.int32, (peers, ROWS, LANES), 2)
    first = lane - ROWS * lax.broadcasted_iota(jnp.int32, (peers, ROWS, LANES), 1)
    tops, totals = [], []
    for head in range(heads):
        row = jnp.broadcast_to(stats[:, head : head + 1, :], (peers, ROWS, LANES))
        tops.append(
            jnp.sum(jnp.where((first >= 0) & (first < 3), row, 0.0), axis=2, keepdims=True)
        )
        totals.append(
            jnp.sum(jnp.where((first >= 3) & (first < 6), row, 0.0), axis=2, keepdims=True)
        )
    top = jnp.concatenate(tops, axis=1)
    total = jnp.concatenate(totals, axis=1)
    peak = jnp.max(top, axis=0, keepdims=True)
    share = total * jnp.exp(top - peak)
    denominator = jnp.sum(share, axis=0)
    columns = []
    for tile in range(tiles):
        piece = got[:, tile * chunk : (tile + 1) * chunk, :].astype(F32)
        columns.append(jnp.sum(piece * share, axis=0) / denominator)
    merged = jnp.concatenate(columns, axis=1)
    values = []
    for head in range(heads):
        rows = merged[ROWS * head : ROWS * (head + 1)].astype(BF16)
        values.append(jnp.dot(rows, value[head], preferred_element_type=F32))
    head_values = jnp.concatenate(values, axis=1).astype(BF16)

    back = jnp.concatenate(
        [ref[...].astype(F32) for ref in (back_0, back_1, back_2, back_3)], axis=0
    ).astype(BF16)
    mixing = mix[...][:, : 4 * CAP]
    high = mixing.astype(BF16)
    low = (mixing - high.astype(F32)).astype(BF16)
    routed = jnp.dot(high, back, preferred_element_type=F32) + jnp.dot(
        low, back, preferred_element_type=F32
    )
    copy.wait()
    attended = jnp.dot(head_values, project_in[...], preferred_element_type=F32)
    both = jnp.concatenate([attended, routed], axis=0)
    span = keep.shape[2]
    for peer in range(peers):
        even = both[:, 2 * peer * span : (2 * peer + 1) * span]
        odd = both[:, (2 * peer + 1) * span : (2 * peer + 2) * span]
        keep[peer] = jnp.where(core == 1, odd, even).astype(BF16)
        send[peer] = jnp.where(core == 1, even, odd).astype(BF16)


def merge(got, value, project, mix, back, span):
    peers = got.shape[0]
    depth, width = project.shape
    shape = jax.ShapeDtypeStruct((peers, 2 * ROWS, span), BF16)
    return pl.pallas_call(
        merge_kernel,
        out_shape=[shape, shape],
        in_specs=[VMEM, VMEM, HBM, VMEM] + [VMEM] * 4,
        out_specs=[VMEM] * 2,
        scratch_shapes=[pltpu.VMEM((depth, width), BF16), pltpu.SemaphoreType.DMA],
        compiler_params=params(24),
        cost_estimate=pl.CostEstimate(
            flops=2 * 8 * depth * width, bytes_accessed=6 * 2**20, transcendentals=0
        ),
        name="merge",
    )(got, value, project, mix, *back)


def shards(
    query_lat,
    query_rope,
    cache_lat,
    cache_rope,
    lengths,
    w_value,
    w_out,
    moe_tokens,
    expert_ids,
    route_weights,
    w_gate,
    w_up,
    w_down,
):
    plane = ("y", "z")
    group_count = lax.axis_size("x")
    peers = lax.axis_size(plane)
    requests = cache_lat.shape[0]
    span = moe_tokens.shape[1]
    swap = [(0, 1), (1, 0)]

    def along_x(value, shift):
        return lax.ppermute(
            value, "x", [(i, (i + shift) % group_count) for i in range(group_count)]
        )

    query = lax.all_to_all(
        payload(query_lat, query_rope, moe_tokens, peers), plane, 0, 0, tiled=True
    )
    lat_far = lax.ppermute(cache_lat, "c", swap)
    rope_far = lax.ppermute(cache_rope, "c", swap)
    scale = (w_value.shape[2] + query_rope.shape[2]) ** (-0.5)
    part, *send, mix = attention(
        lengths,
        query,
        cache_lat,
        lat_far,
        cache_rope,
        rope_far,
        expert_ids,
        route_weights,
        scale,
        span,
        w_gate.shape[1],
    )
    got = lax.all_to_all(part, plane, 0, 0, tiled=True)

    near = [send[0]] + [along_x(send[d], d) for d in range(1, group_count)]
    own = jnp.concatenate(near, axis=0)
    far = lax.ppermute(own, "c", swap)
    routed = experts(own, far, w_gate, w_up, w_down)
    back = [routed[0]] + [along_x(routed[d], -d) for d in range(1, group_count)]

    keep, give = merge(got, w_value, w_out, mix, back, span)
    taken = lax.ppermute(give, "c", swap)
    terms = (keep.astype(F32) + taken.astype(F32)).astype(BF16)
    arrived = lax.all_to_all(terms, plane, 0, 0, tiled=True)
    summed = jnp.sum(arrived.astype(F32), axis=0).astype(BF16)
    return (summed[:requests], summed[requests:])


def solution(mesh):
    groups = mesh.shape["grp"]
    split = Mesh(mesh.devices.reshape(groups, 4, 8, 2), ("x",) + KV)
    both = ("x",) + KV
    return jax.shard_map(
        shards,
        mesh=split,
        in_specs=(
            P("x", KV, None),
            P("x", KV, None),
            P("x", KV, None),
            P("x", None, KV),
            P("x"),
            P(KV, None, None),
            P(KV, None),
            P("x", KV),
            P("x", None),
            P("x", None),
            P(None, both),
            P(None, both),
            P(both, None),
        ),
        out_specs=(P("x", KV), P("x", KV)),
        check_vma=False,
    )
```

```python
import jax
import jax.numpy as jnp
from jax import lax
from jax.experimental import pallas as pl
from jax.experimental.pallas import tpu as pltpu
from jax.sharding import Mesh
from jax.sharding import PartitionSpec as P

FF = 1024
CAP = 4
ROWS = 8
F32 = jnp.float32
BF16 = jnp.bfloat16
LANES = 128
KV = ("y", "z", "c")
VMEM = pl.BlockSpec(memory_space=pltpu.VMEM)
SMEM = pl.BlockSpec(memory_space=pltpu.SMEM)
HBM = pl.BlockSpec(memory_space=pltpu.HBM)


def three_terms(value):
    high = value.astype(BF16).astype(F32)
    rest = value - high
    middle = rest.astype(BF16).astype(F32)
    return high, middle, rest - middle


def pinned(*values):
    return [pltpu.with_memory_space_constraint(value, pltpu.HBM) for value in values]


def params(mebibytes):
    return pltpu.CompilerParams(vmem_limit_bytes=mebibytes * 2**20)


def payload_kernel(query_lat, query_rope, tokens, out):
    peers = out.shape[0]
    latent, rope = query_lat.shape[2], query_rope.shape[2]
    heads = query_lat.shape[1]
    half = tokens.shape[1] // heads
    lat = query_lat[...].astype(F32)
    rot = query_rope[...].astype(F32)
    tok = tokens[...].astype(F32)
    spare = jnp.zeros((ROWS, out.shape[2] - latent - rope - half), F32)
    rows = []
    for head in range(heads):
        tail = jnp.concatenate(
            [rot[:, head, :], tok[:, head * half : (head + 1) * half], spare], axis=1
        )
        rows.append(jnp.concatenate([lat[:, head, :], tail], axis=1))
    chunk = jnp.concatenate(rows, axis=0).astype(BF16)
    for peer in range(peers):
        out[peer] = chunk


def payload(query_lat, query_rope, tokens, peers):
    requests, heads, latent = query_lat.shape
    return pl.pallas_call(
        payload_kernel,
        out_shape=jax.ShapeDtypeStruct((peers, heads * requests, latent + LANES), BF16),
        in_specs=[VMEM] * 3,
        out_specs=VMEM,
        compiler_params=params(20),
        name="payload",
    )(*pinned(query_lat, query_rope, tokens))


def attention_kernel(
    lengths,
    query,
    lat_own,
    lat_far,
    rope_own,
    rope_far,
    ids,
    route,
    out,
    send_0,
    send_1,
    send_2,
    send_3,
    mix_out,
    query_rows,
    out_rows,
    stat_rows,
    token_rows,
    lengths_in,
    lat_in,
    rope_in,
    ids_in,
    route_in,
    sems,
    *,
    scale,
    units,
):
    peers, chunk, width = query.shape
    requests, positions, latent = lat_own.shape
    small = [
        pltpu.make_async_copy(lengths, lengths_in, sems.at[requests]),
        pltpu.make_async_copy(rope_own, rope_in, sems.at[requests + 1]),
        pltpu.make_async_copy(ids, ids_in, sems.at[requests + 2]),
        pltpu.make_async_copy(route, route_in, sems.at[requests + 3]),
    ]
    large = [
        pltpu.make_async_copy(lat_own.at[request], lat_in.at[request], sems.at[request])
        for request in range(requests)
    ]
    for copy in small[:2] + large + small[2:]:
        copy.start()
    rope = rope_own.shape[1]
    tiles = latent // LANES
    heads = chunk // requests
    group, groups = lax.axis_index("x"), lax.axis_size("x")
    shard, shards_here = lax.axis_index(KV), lax.axis_size(KV)
    core = lax.axis_index("c")
    rows = peers * heads

    for tile in range(tiles + 1):
        piece = query[:, :, tile * LANES : (tile + 1) * LANES].astype(F32)
        query_rows[tile] = piece.reshape(peers * chunk, LANES)

    lane = lax.broadcasted_iota(jnp.int32, (rows, LANES), 1)
    stats = jnp.zeros((rows, LANES), F32)
    base_own = shard * positions
    base_far = (shard + 1 - 2 * core) * positions
    place = lax.broadcasted_iota(jnp.int32, (rows, positions), 1)
    small[0].wait()
    for request in range(requests):
        if request == 0:
            small[1].wait()
        large[request].wait()
        mine = jnp.concatenate(
            [
                jnp.concatenate(
                    [
                        query_rows[tile, pl.ds(requests * head + request, peers, stride=chunk), :]
                        for tile in range(tiles + 1)
                    ],
                    axis=1,
                )
                for head in range(heads)
            ],
            axis=0,
        ).astype(BF16)
        length = lengths_in[request]
        parts = []
        for lat, rot, base in ((lat_in, rope_in, base_own), (lat_far, rope_far, base_far)):
            score = (
                lax.dot_general(
                    mine[:, :latent],
                    lat[request],
                    (((1,), (1,)), ((), ())),
                    preferred_element_type=F32,
                )
                + jnp.dot(
                    mine[:, latent : latent + rope], rot[request], preferred_element_type=F32
                )
            ) * scale
            usable = place < length - base
            parts.append((jnp.where(usable, score, -1e30), usable, lat))
        top = jnp.max(jnp.maximum(parts[0][0], parts[1][0]), axis=1, keepdims=True)
        weights = [jnp.where(usable, jnp.exp(score - top), 0.0) for score, usable, _ in parts]
        total = jnp.sum(weights[0] + weights[1], axis=1, keepdims=True)
        weighted = jnp.dot(
            weights[0].astype(BF16), lat_in[request], preferred_element_type=F32
        ) + jnp.dot(weights[1].astype(BF16), lat_far[request], preferred_element_type=F32)
        partial = weighted / jnp.maximum(total, 1.0)
        for index, term in enumerate(three_terms(top) + three_terms(total)):
            stats = jnp.where(lane == ROWS * request + index, term, stats)
        for head in range(heads):
            for tile in range(tiles):
                out_rows[tile, pl.ds(requests * head + request, peers, stride=chunk), :] = partial[
                    peers * head : peers * (head + 1), tile * LANES : (tile + 1) * LANES
                ]

    for tile in range(tiles):
        out[:, tile * chunk : (tile + 1) * chunk, :] = (
            out_rows[tile].reshape(peers, chunk, LANES).astype(BF16)
        )
    stat_rows[...] = jnp.zeros_like(stat_rows)
    for head in range(heads):
        stat_rows[pl.ds(head, peers, stride=ROWS), :] = stats[peers * head : peers * (head + 1)]
    out[:, tiles * chunk :, :] = stat_rows[...].reshape(peers, ROWS, LANES).astype(BF16)

    half = token_rows.shape[1] // (peers * heads)
    for peer in range(peers):
        begin = peer * chunk
        pieces = [
            query_rows[tiles, begin + requests * head : begin + requests * (head + 1), :][
                :, rope : rope + half
            ]
            for head in range(heads)
        ]
        token_rows[:, peer * heads * half : (peer + 1) * heads * half] = jnp.concatenate(
            pieces, axis=1
        )
    tokens = token_rows[...].astype(BF16)
    small[2].wait()
    small[3].wait()
    named = ids_in[...]
    strength = route_in[...]
    lower = (
        lax.broadcasted_iota(jnp.int32, (ROWS, ROWS), 1)
        < lax.broadcasted_iota(jnp.int32, (ROWS, ROWS), 0)
    ).astype(F32)
    slot_lane = lax.broadcasted_iota(jnp.int32, (ROWS, LANES), 1)
    placing = jnp.zeros((ROWS, LANES), F32)
    mix = jnp.zeros((ROWS, LANES), F32)
    for step in range(4):
        expert = (lax.rem(group + step, groups) * shards_here + shard) * units // FF
        hit = named == expert
        chosen = jnp.max(jnp.where(hit, 1.0, 0.0), axis=1, keepdims=True)
        weight = jnp.sum(jnp.where(hit, strength, 0.0), axis=1, keepdims=True)
        chosen_wide = jnp.broadcast_to(chosen, (ROWS, LANES))
        rank = jnp.dot(lower, chosen_wide, preferred_element_type=F32)
        picked = (rank == (slot_lane - CAP * step).astype(F32)) & (chosen_wide > 0.0)
        picked = picked & (slot_lane >= CAP * step) & (slot_lane < CAP * (step + 1))
        placing = jnp.where(picked, 1.0, placing)
        mix = jnp.where(picked, weight, mix)
    mix_out[...] = mix
    select = placing.T[: 4 * CAP, :].astype(BF16)
    chosen_rows = jnp.dot(select, tokens, preferred_element_type=F32).astype(BF16)
    for step, send in enumerate((send_0, send_1, send_2, send_3)):
        send[...] = chosen_rows[CAP * step : CAP * (step + 1)]


def attention(lengths, query, lat_own, lat_far, rope_own, rope_far, ids, route, scale, span, units):
    peers, chunk, width = query.shape
    requests, positions, latent = lat_own.shape
    rope = rope_own.shape[1]
    tiles = latent // LANES
    lengths, lat_own, rope_own, ids, route = pinned(lengths, lat_own, rope_own, ids, route)
    return pl.pallas_call(
        lambda *refs: attention_kernel(*refs, scale=scale, units=units),
        out_shape=[jax.ShapeDtypeStruct((peers, tiles * chunk + ROWS, LANES), BF16)]
        + [jax.ShapeDtypeStruct((CAP, peers * span), BF16)] * 4
        + [jax.ShapeDtypeStruct((ROWS, LANES), F32)],
        in_specs=[HBM, VMEM, HBM, VMEM, HBM, VMEM, HBM, HBM],
        out_specs=[VMEM] * 6,
        scratch_shapes=[
            pltpu.VMEM((width // LANES, peers * chunk, LANES), F32),
            pltpu.VMEM((tiles, peers * chunk, LANES), F32),
            pltpu.VMEM((peers * ROWS, LANES), F32),
            pltpu.VMEM((requests, peers * span), F32),
            pltpu.SMEM(lengths.shape, jnp.int32),
            pltpu.VMEM(lat_own.shape, BF16),
            pltpu.VMEM(rope_own.shape, BF16),
            pltpu.VMEM(ids.shape, jnp.int32),
            pltpu.VMEM(route.shape, F32),
            pltpu.SemaphoreType.DMA((requests + 4,)),
        ],
        compiler_params=params(24),
        cost_estimate=pl.CostEstimate(
            flops=2 * peers * chunk * 2 * positions * (2 * latent + rope),
            bytes_accessed=6 * 2**20,
            transcendentals=peers * chunk * 2 * positions,
        ),
        name="attention",
    )(lengths, query, lat_own, lat_far, rope_own, rope_far, ids, route)


def fetch_kernel(after, *refs):
    del after
    count = len(refs) // 2
    sems = refs[-1]
    copies = [
        pltpu.make_async_copy(refs[index], refs[count + index], sems.at[index])
        for index in range(count)
    ]
    for copy in copies:
        copy.start()
    for copy in copies:
        copy.wait()


def fetch(after, *weights):
    return pl.pallas_call(
        fetch_kernel,
        out_shape=[pltpu.VMEM(weight.shape, weight.dtype) for weight in weights],
        in_specs=[pl.BlockSpec(memory_space=pl.ANY)] + [HBM] * len(weights),
        out_specs=[VMEM] * len(weights),
        scratch_shapes=[pltpu.SemaphoreType.DMA((len(weights),))],
        compiler_params=params(1),
        cost_estimate=pl.CostEstimate(flops=0, bytes_accessed=10 * 2**20, transcendentals=0),
        name="fetch",
    )(after, *pinned(*weights))


def experts_kernel(own, far, gate, up, down, keep, send):
    depth, units = gate.shape
    width = down.shape[1]
    span = 112
    blocks = depth // (2 * span)
    core = lax.axis_index("c")
    each = 8
    total = jnp.zeros((own.shape[0], 2 * units), F32)
    for index in range(blocks // each):
        for tokens, parity in ((own, core), (far, 1 - core)):
            columns = []
            for source in (gate, up):
                columns.append(
                    jnp.concatenate(
                        [
                            source[
                                pl.ds(
                                    pl.multiple_of(2 * span * block + span * parity, 16), span
                                ),
                                :,
                            ]
                            for block in range(each * index, each * (index + 1))
                        ],
                        axis=0,
                    )
                )
            total += jnp.dot(
                tokens[:, each * span * index : each * span * (index + 1)],
                jnp.concatenate(columns, axis=1),
                preferred_element_type=F32,
            )
    gate_proj, up_proj = total[:, :units], total[:, units:]
    hidden = (gate_proj * jax.nn.sigmoid(gate_proj) * up_proj).astype(BF16)
    pair = 2 * span
    step = 8 * span
    for start in range(0, width, step):
        result = jnp.dot(hidden, down[:, start : start + step], preferred_element_type=F32)
        evens, odds = [], []
        for inner in range(0, step, pair):
            evens.append(result[:, inner : inner + span])
            odds.append(result[:, inner + span : inner + pair])
        even, odd = jnp.concatenate(evens, axis=1), jnp.concatenate(odds, axis=1)
        here = slice(start // 2, (start + step) // 2)
        keep[:, here] = jnp.where(core == 1, odd, even)
        send[:, here] = jnp.where(core == 1, even, odd).astype(BF16)


def experts(own, far, gate, up, down):
    depth, units = gate.shape
    width = down.shape[1]
    shape = (own.shape[0], width // 2)
    return pl.pallas_call(
        experts_kernel,
        out_shape=[jax.ShapeDtypeStruct(shape, F32), jax.ShapeDtypeStruct(shape, BF16)],
        in_specs=[VMEM] * 5,
        out_specs=[VMEM] * 2,
        compiler_params=params(16),
        cost_estimate=pl.CostEstimate(
            flops=2 * 16 * 3 * depth * units, bytes_accessed=6 * 2**20, transcendentals=0
        ),
        name="experts",
    )(own, far, gate, up, down)


def pair_kernel(keep, taken, *outs):
    total = (keep[...] + taken[...].astype(F32)).astype(BF16)
    for block, out in enumerate(outs):
        out[...] = total[CAP * block : CAP * (block + 1)]


def pair(keep, taken):
    width = keep.shape[1]
    return pl.pallas_call(
        pair_kernel,
        out_shape=[jax.ShapeDtypeStruct((CAP, width), BF16)] * 4,
        in_specs=[VMEM] * 2,
        out_specs=[VMEM] * 4,
        compiler_params=params(8),
        name="pair",
    )(keep, taken)


def merge_kernel(got, value, project, keep, send):
    peers, height, _ = got.shape
    heads = value.shape[0]
    chunk = ROWS * heads
    tiles = height // chunk
    core = lax.axis_index("c")
    stats = got[:, tiles * chunk :, :].astype(F32)
    lane = lax.broadcasted_iota(jnp.int32, (peers, ROWS, LANES), 2)
    first = lane - ROWS * lax.broadcasted_iota(jnp.int32, (peers, ROWS, LANES), 1)
    tops, totals = [], []
    for head in range(heads):
        row = jnp.broadcast_to(stats[:, head : head + 1, :], (peers, ROWS, LANES))
        tops.append(
            jnp.sum(jnp.where((first >= 0) & (first < 3), row, 0.0), axis=2, keepdims=True)
        )
        totals.append(
            jnp.sum(jnp.where((first >= 3) & (first < 6), row, 0.0), axis=2, keepdims=True)
        )
    top = jnp.concatenate(tops, axis=1)
    total = jnp.concatenate(totals, axis=1)
    peak = jnp.max(top, axis=0, keepdims=True)
    share = total * jnp.exp(top - peak)
    denominator = jnp.sum(share, axis=0)
    columns = []
    for tile in range(tiles):
        piece = got[:, tile * chunk : (tile + 1) * chunk, :].astype(F32)
        columns.append(jnp.sum(piece * share, axis=0) / denominator)
    merged = jnp.concatenate(columns, axis=1)
    values = []
    for head in range(heads):
        rows = merged[ROWS * head : ROWS * (head + 1)].astype(BF16)
        values.append(jnp.dot(rows, value[head], preferred_element_type=F32))
    head_values = jnp.concatenate(values, axis=1).astype(BF16)
    attended = jnp.dot(head_values, project[...], preferred_element_type=F32)
    span = keep.shape[2]
    for peer in range(peers):
        even = attended[:, 2 * peer * span : (2 * peer + 1) * span]
        odd = attended[:, (2 * peer + 1) * span : (2 * peer + 2) * span]
        keep[peer] = jnp.where(core == 1, odd, even)
        send[peer] = jnp.where(core == 1, even, odd).astype(BF16)


def merge(got, value, project, span):
    peers = got.shape[0]
    depth, width = project.shape
    shape = (peers, ROWS, span)
    return pl.pallas_call(
        merge_kernel,
        out_shape=[jax.ShapeDtypeStruct(shape, F32), jax.ShapeDtypeStruct(shape, BF16)],
        in_specs=[VMEM] * 3,
        out_specs=[VMEM] * 2,
        compiler_params=params(16),
        cost_estimate=pl.CostEstimate(
            flops=2 * 8 * depth * width, bytes_accessed=6 * 2**20, transcendentals=0
        ),
        name="merge",
    )(got, value, project)


def finish_kernel(keep, taken, mix, back_0, back_1, back_2, back_3, out):
    peers, _, span = keep.shape
    back = jnp.concatenate(
        [ref[...].astype(F32) for ref in (back_0, back_1, back_2, back_3)], axis=0
    ).astype(BF16)
    mixing = mix[...][:, : 4 * CAP]
    high = mixing.astype(BF16)
    low = (mixing - high.astype(F32)).astype(BF16)
    routed = jnp.dot(high, back, preferred_element_type=F32) + jnp.dot(
        low, back, preferred_element_type=F32
    )
    for peer in range(peers):
        attended = keep[peer] + taken[peer].astype(F32)
        both = jnp.concatenate([attended, routed[:, peer * span : (peer + 1) * span]], axis=0)
        out[peer] = both.astype(BF16)


def finish(keep, taken, mix, back):
    peers, rows, span = keep.shape
    return pl.pallas_call(
        finish_kernel,
        out_shape=jax.ShapeDtypeStruct((peers, 2 * rows, span), BF16),
        in_specs=[VMEM] * 7,
        out_specs=VMEM,
        compiler_params=params(8),
        name="finish",
    )(keep, taken, mix, *back)


def shards(
    query_lat,
    query_rope,
    cache_lat,
    cache_rope,
    lengths,
    w_value,
    w_out,
    moe_tokens,
    expert_ids,
    route_weights,
    w_gate,
    w_up,
    w_down,
):
    plane = ("y", "z")
    group_count = lax.axis_size("x")
    peers = lax.axis_size(plane)
    requests = cache_lat.shape[0]
    span = moe_tokens.shape[1]
    swap = [(0, 1), (1, 0)]

    def along_x(value, shift):
        return lax.ppermute(
            value, "x", [(i, (i + shift) % group_count) for i in range(group_count)]
        )

    query = lax.all_to_all(
        payload(query_lat, query_rope, moe_tokens, peers), plane, 0, 0, tiled=True
    )
    lat_far = lax.ppermute(cache_lat, "c", swap)
    rope_far = lax.ppermute(cache_rope, "c", swap)
    scale = (w_value.shape[2] + query_rope.shape[2]) ** (-0.5)
    part, *send, mix = attention(
        lengths,
        query,
        cache_lat,
        lat_far,
        cache_rope,
        rope_far,
        expert_ids,
        route_weights,
        scale,
        span,
        w_gate.shape[1],
    )
    got = lax.all_to_all(part, plane, 0, 0, tiled=True)

    near = [send[0]] + [along_x(send[d], d) for d in range(1, group_count)]
    own = jnp.concatenate(near, axis=0)
    far = lax.ppermute(own, "c", swap)
    gate, up, down, project, value = fetch(part, w_gate, w_up, w_down, w_out, w_value)
    keep, give = experts(own, far, gate, up, down)
    routed = pair(keep, lax.ppermute(give, "c", swap))
    back = [routed[0]] + [along_x(routed[d], -d) for d in range(1, group_count)]

    keep, give = merge(got, value, project, span)
    terms = finish(keep, lax.ppermute(give, "c", swap), mix, back)
    arrived = lax.all_to_all(terms, plane, 0, 0, tiled=True)
    summed = jnp.sum(arrived.astype(F32), axis=0).astype(BF16)
    return (summed[:requests], summed[requests:])


def solution(mesh):
    groups = mesh.shape["grp"]
    split = Mesh(mesh.devices.reshape(groups, 4, 8, 2), ("x",) + KV)
    both = ("x",) + KV
    return jax.shard_map(
        shards,
        mesh=split,
        in_specs=(
            P("x", KV, None),
            P("x", KV, None),
            P("x", KV, None),
            P("x", None, KV),
            P("x"),
            P(KV, None, None),
            P(KV, None),
            P("x", KV),
            P("x", None),
            P("x", None),
            P(None, both),
            P(None, both),
            P(both, None),
        ),
        out_specs=(P("x", KV), P("x", KV)),
        check_vma=False,
    )
```

```python
import jax
import jax.numpy as jnp
from jax import lax
from jax.experimental import pallas as pl
from jax.experimental.pallas import tpu as pltpu
from jax.sharding import Mesh
from jax.sharding import PartitionSpec as P

FF = 1024
CAP = 4
ROWS = 8
F32 = jnp.float32
BF16 = jnp.bfloat16
LANES = 128
KV = ("y", "z", "c")
VMEM = pl.BlockSpec(memory_space=pltpu.VMEM)
SMEM = pl.BlockSpec(memory_space=pltpu.SMEM)
HBM = pl.BlockSpec(memory_space=pltpu.HBM)


def three_terms(value):
    high = value.astype(BF16).astype(F32)
    rest = value - high
    middle = rest.astype(BF16).astype(F32)
    return high, middle, rest - middle


def pinned(*values):
    return [pltpu.with_memory_space_constraint(value, pltpu.HBM) for value in values]


def params(mebibytes):
    return pltpu.CompilerParams(vmem_limit_bytes=mebibytes * 2**20)


def payload_kernel(query_lat, query_rope, tokens, out, lat_in, rope_in, tokens_in, sems):
    copies = [
        pltpu.make_async_copy(source, target, sems.at[index])
        for index, (source, target) in enumerate(
            ((query_lat, lat_in), (query_rope, rope_in), (tokens, tokens_in))
        )
    ]
    for copy in copies:
        copy.start()
    for copy in copies:
        copy.wait()
    peers = out.shape[0]
    latent, rope = query_lat.shape[2], query_rope.shape[2]
    heads = query_lat.shape[1]
    half = tokens.shape[1] // heads
    lat = lat_in[...].astype(F32)
    rot = rope_in[...].astype(F32)
    tok = tokens_in[...].astype(F32)
    spare = jnp.zeros((ROWS, out.shape[2] - latent - rope - half), F32)
    rows = []
    for head in range(heads):
        tail = jnp.concatenate(
            [rot[:, head, :], tok[:, head * half : (head + 1) * half], spare], axis=1
        )
        rows.append(jnp.concatenate([lat[:, head, :], tail], axis=1))
    chunk = jnp.concatenate(rows, axis=0).astype(BF16)
    for peer in range(peers):
        out[peer] = chunk


def payload(query_lat, query_rope, tokens, peers):
    requests, heads, latent = query_lat.shape
    return pl.pallas_call(
        payload_kernel,
        out_shape=jax.ShapeDtypeStruct((peers, heads * requests, latent + LANES), BF16),
        in_specs=[HBM] * 3,
        out_specs=VMEM,
        scratch_shapes=[
            pltpu.VMEM(query_lat.shape, BF16),
            pltpu.VMEM(query_rope.shape, BF16),
            pltpu.VMEM(tokens.shape, BF16),
            pltpu.SemaphoreType.DMA((3,)),
        ],
        compiler_params=params(20),
        name="payload",
    )(*pinned(query_lat, query_rope, tokens))


def attention_kernel(
    lengths,
    query,
    lat_own,
    lat_far,
    rope_own,
    rope_far,
    ids,
    route,
    out,
    send_0,
    send_1,
    send_2,
    send_3,
    mix_out,
    query_rows,
    out_rows,
    stat_rows,
    token_rows,
    lengths_in,
    lat_in,
    rope_in,
    ids_in,
    route_in,
    sems,
    *,
    scale,
    units,
):
    peers, chunk, width = query.shape
    requests, positions, latent = lat_own.shape
    small = [
        pltpu.make_async_copy(lengths, lengths_in, sems.at[0]),
        pltpu.make_async_copy(rope_own, rope_in, sems.at[1]),
        pltpu.make_async_copy(ids, ids_in, sems.at[2]),
        pltpu.make_async_copy(route, route_in, sems.at[3]),
    ]
    large = pltpu.make_async_copy(lat_own, lat_in, sems.at[4])
    for copy in small[2:] + small[:2] + [large]:
        copy.start()
    rope = rope_own.shape[1]
    tiles = latent // LANES
    heads = chunk // requests
    group, groups = lax.axis_index("x"), lax.axis_size("x")
    shard, shards_here = lax.axis_index(KV), lax.axis_size(KV)
    core = lax.axis_index("c")
    rows = peers * heads

    for tile in range(tiles + 1):
        piece = query[:, :, tile * LANES : (tile + 1) * LANES].astype(F32)
        query_rows[tile] = piece.reshape(peers * chunk, LANES)

    half = token_rows.shape[1] // (peers * heads)
    for peer in range(peers):
        begin = peer * chunk
        pieces = [
            query_rows[tiles, begin + requests * head : begin + requests * (head + 1), :][
                :, rope : rope + half
            ]
            for head in range(heads)
        ]
        token_rows[:, peer * heads * half : (peer + 1) * heads * half] = jnp.concatenate(
            pieces, axis=1
        )
    tokens = token_rows[...].astype(BF16)
    small[2].wait()
    small[3].wait()
    named = ids_in[...]
    strength = route_in[...]
    lower = (
        lax.broadcasted_iota(jnp.int32, (ROWS, ROWS), 1)
        < lax.broadcasted_iota(jnp.int32, (ROWS, ROWS), 0)
    ).astype(F32)
    slot_lane = lax.broadcasted_iota(jnp.int32, (ROWS, LANES), 1)
    placing = jnp.zeros((ROWS, LANES), F32)
    mix = jnp.zeros((ROWS, LANES), F32)
    for step in range(4):
        expert = (lax.rem(group + step, groups) * shards_here + shard) * units // FF
        hit = named == expert
        chosen = jnp.max(jnp.where(hit, 1.0, 0.0), axis=1, keepdims=True)
        weight = jnp.sum(jnp.where(hit, strength, 0.0), axis=1, keepdims=True)
        chosen_wide = jnp.broadcast_to(chosen, (ROWS, LANES))
        rank = jnp.dot(lower, chosen_wide, preferred_element_type=F32)
        picked = (rank == (slot_lane - CAP * step).astype(F32)) & (chosen_wide > 0.0)
        picked = picked & (slot_lane >= CAP * step) & (slot_lane < CAP * (step + 1))
        placing = jnp.where(picked, 1.0, placing)
        mix = jnp.where(picked, weight, mix)
    mix_out[...] = mix
    select = placing.T[: 4 * CAP, :].astype(BF16)
    chosen_rows = jnp.dot(select, tokens, preferred_element_type=F32).astype(BF16)
    for step, send in enumerate((send_0, send_1, send_2, send_3)):
        send[...] = chosen_rows[CAP * step : CAP * (step + 1)]

    lane = lax.broadcasted_iota(jnp.int32, (rows, LANES), 1)
    stats = jnp.zeros((rows, LANES), F32)
    base_own = shard * positions
    base_far = (shard + 1 - 2 * core) * positions
    place = lax.broadcasted_iota(jnp.int32, (rows, positions), 1)
    small[0].wait()
    small[1].wait()
    large.wait()
    for request in range(requests):
        mine = jnp.concatenate(
            [
                jnp.concatenate(
                    [
                        query_rows[tile, pl.ds(requests * head + request, peers, stride=chunk), :]
                        for tile in range(tiles + 1)
                    ],
                    axis=1,
                )
                for head in range(heads)
            ],
            axis=0,
        ).astype(BF16)
        length = lengths_in[request]
        parts = []
        for lat, rot, base in ((lat_in, rope_in, base_own), (lat_far, rope_far, base_far)):
            score = (
                lax.dot_general(
                    mine[:, :latent],
                    lat[request],
                    (((1,), (1,)), ((), ())),
                    preferred_element_type=F32,
                )
                + jnp.dot(
                    mine[:, latent : latent + rope], rot[request], preferred_element_type=F32
                )
            ) * scale
            usable = place < length - base
            parts.append((jnp.where(usable, score, -1e30), usable, lat))
        top = jnp.max(jnp.maximum(parts[0][0], parts[1][0]), axis=1, keepdims=True)
        weights = [jnp.where(usable, jnp.exp(score - top), 0.0) for score, usable, _ in parts]
        total = jnp.sum(weights[0] + weights[1], axis=1, keepdims=True)
        weighted = jnp.dot(
            weights[0].astype(BF16), lat_in[request], preferred_element_type=F32
        ) + jnp.dot(weights[1].astype(BF16), lat_far[request], preferred_element_type=F32)
        partial = weighted * (1.0 / jnp.maximum(total, 1.0))
        for index, term in enumerate(three_terms(top) + three_terms(total)):
            stats = jnp.where(lane == ROWS * request + index, term, stats)
        for head in range(heads):
            for tile in range(tiles):
                out_rows[tile, pl.ds(requests * head + request, peers, stride=chunk), :] = partial[
                    peers * head : peers * (head + 1), tile * LANES : (tile + 1) * LANES
                ]

    for tile in range(tiles):
        out[:, tile * chunk : (tile + 1) * chunk, :] = (
            out_rows[tile].reshape(peers, chunk, LANES).astype(BF16)
        )
    stat_rows[...] = jnp.zeros_like(stat_rows)
    for head in range(heads):
        stat_rows[pl.ds(head, peers, stride=ROWS), :] = stats[peers * head : peers * (head + 1)]
    out[:, tiles * chunk :, :] = stat_rows[...].reshape(peers, ROWS, LANES).astype(BF16)


def attention(lengths, query, lat_own, lat_far, rope_own, rope_far, ids, route, scale, span, units):
    peers, chunk, width = query.shape
    requests, positions, latent = lat_own.shape
    rope = rope_own.shape[1]
    tiles = latent // LANES
    lengths, lat_own, rope_own, ids, route = pinned(lengths, lat_own, rope_own, ids, route)
    return pl.pallas_call(
        lambda *refs: attention_kernel(*refs, scale=scale, units=units),
        out_shape=[jax.ShapeDtypeStruct((peers, tiles * chunk + ROWS, LANES), BF16)]
        + [jax.ShapeDtypeStruct((CAP, peers * span), BF16)] * 4
        + [jax.ShapeDtypeStruct((ROWS, LANES), F32)],
        in_specs=[HBM, VMEM, HBM, VMEM, HBM, VMEM, HBM, HBM],
        out_specs=[VMEM] * 6,
        scratch_shapes=[
            pltpu.VMEM((width // LANES, peers * chunk, LANES), F32),
            pltpu.VMEM((tiles, peers * chunk, LANES), F32),
            pltpu.VMEM((peers * ROWS, LANES), F32),
            pltpu.VMEM((requests, peers * span), F32),
            pltpu.SMEM(lengths.shape, jnp.int32),
            pltpu.VMEM(lat_own.shape, BF16),
            pltpu.VMEM(rope_own.shape, BF16),
            pltpu.VMEM(ids.shape, jnp.int32),
            pltpu.VMEM(route.shape, F32),
            pltpu.SemaphoreType.DMA((5,)),
        ],
        compiler_params=params(24),
        cost_estimate=pl.CostEstimate(
            flops=2 * peers * chunk * 2 * positions * (2 * latent + rope),
            bytes_accessed=6 * 2**20,
            transcendentals=peers * chunk * 2 * positions,
        ),
        name="attention",
    )(lengths, query, lat_own, lat_far, rope_own, rope_far, ids, route)


def experts_kernel(own, far, gate, up, down, keep, send, gate_in, up_in, down_in, sems):
    depth, units = gate.shape
    width = down.shape[1]
    span = 112
    blocks = depth // (2 * span)
    core = lax.axis_index("c")
    each = 8
    copies = []
    for index in range(blocks // each):
        rows = pl.ds(2 * span * each * index, 2 * span * each)
        copies.append(
            [
                pltpu.make_async_copy(
                    source.at[rows, :], target.at[rows, :], sems.at[2 * index + number]
                )
                for number, (source, target) in enumerate(((gate, gate_in), (up, up_in)))
            ]
        )
    last = pltpu.make_async_copy(down, down_in, sems.at[2 * blocks // each])
    for copy in sum(copies, []) + [last]:
        copy.start()
    total = jnp.zeros((own.shape[0], 2 * units), F32)
    for index in range(blocks // each):
        for copy in copies[index]:
            copy.wait()
        for tokens, parity in ((own, core), (far, 1 - core)):
            columns = []
            for source in (gate_in, up_in):
                columns.append(
                    jnp.concatenate(
                        [
                            source[
                                pl.ds(
                                    pl.multiple_of(2 * span * block + span * parity, 16), span
                                ),
                                :,
                            ]
                            for block in range(each * index, each * (index + 1))
                        ],
                        axis=0,
                    )
                )
            total += jnp.dot(
                tokens[:, each * span * index : each * span * (index + 1)],
                jnp.concatenate(columns, axis=1),
                preferred_element_type=F32,
            )
    gate_proj, up_proj = total[:, :units], total[:, units:]
    hidden = (gate_proj * jax.nn.sigmoid(gate_proj) * up_proj).astype(BF16)
    last.wait()
    pair = 2 * span
    step = 8 * span
    for start in range(0, width, step):
        result = jnp.dot(hidden, down_in[:, start : start + step], preferred_element_type=F32)
        evens, odds = [], []
        for inner in range(0, step, pair):
            evens.append(result[:, inner : inner + span])
            odds.append(result[:, inner + span : inner + pair])
        even, odd = jnp.concatenate(evens, axis=1), jnp.concatenate(odds, axis=1)
        here = slice(start // 2, (start + step) // 2)
        keep[:, here] = jnp.where(core == 1, odd, even)
        send[:, here] = jnp.where(core == 1, even, odd).astype(BF16)


def experts(own, far, gate, up, down):
    depth, units = gate.shape
    width = down.shape[1]
    shape = (own.shape[0], width // 2)
    return pl.pallas_call(
        experts_kernel,
        out_shape=[jax.ShapeDtypeStruct(shape, F32), jax.ShapeDtypeStruct(shape, BF16)],
        in_specs=[VMEM] * 2 + [HBM] * 3,
        out_specs=[VMEM] * 2,
        scratch_shapes=[
            pltpu.VMEM(gate.shape, BF16),
            pltpu.VMEM(up.shape, BF16),
            pltpu.VMEM(down.shape, BF16),
            pltpu.SemaphoreType.DMA((9,)),
        ],
        compiler_params=params(16),
        cost_estimate=pl.CostEstimate(
            flops=2 * 16 * 3 * depth * units, bytes_accessed=6 * 2**20, transcendentals=0
        ),
        name="experts",
    )(own, far, *pinned(gate, up, down))


def pair_kernel(keep, taken, *outs):
    total = (keep[...] + taken[...].astype(F32)).astype(BF16)
    for block, out in enumerate(outs):
        out[...] = total[CAP * block : CAP * (block + 1)]


def pair(keep, taken):
    width = keep.shape[1]
    return pl.pallas_call(
        pair_kernel,
        out_shape=[jax.ShapeDtypeStruct((CAP, width), BF16)] * 4,
        in_specs=[VMEM] * 2,
        out_specs=[VMEM] * 4,
        compiler_params=params(8),
        name="pair",
    )(keep, taken)


def merge_kernel(got, value, project, keep, send, value_in, project_in, sems):
    depth, width = project.shape
    step = 16 * keep.shape[2]
    first_copy = pltpu.make_async_copy(value, value_in, sems.at[width // step])
    first_copy.start()
    copies = []
    for index in range(width // step):
        columns = pl.ds(index * step, step)
        copies.append(
            pltpu.make_async_copy(
                project.at[:, columns], project_in.at[:, columns], sems.at[index]
            )
        )
        copies[index].start()
    peers, height, _ = got.shape
    heads = value.shape[0]
    chunk = ROWS * heads
    tiles = height // chunk
    core = lax.axis_index("c")
    stats = got[:, tiles * chunk :, :].astype(F32)
    lane = lax.broadcasted_iota(jnp.int32, (peers, ROWS, LANES), 2)
    first = lane - ROWS * lax.broadcasted_iota(jnp.int32, (peers, ROWS, LANES), 1)
    tops, totals = [], []
    for head in range(heads):
        row = jnp.broadcast_to(stats[:, head : head + 1, :], (peers, ROWS, LANES))
        tops.append(
            jnp.sum(jnp.where((first >= 0) & (first < 3), row, 0.0), axis=2, keepdims=True)
        )
        totals.append(
            jnp.sum(jnp.where((first >= 3) & (first < 6), row, 0.0), axis=2, keepdims=True)
        )
    top = jnp.concatenate(tops, axis=1)
    total = jnp.concatenate(totals, axis=1)
    peak = jnp.max(top, axis=0, keepdims=True)
    share = total * jnp.exp(top - peak)
    denominator = jnp.sum(share, axis=0)
    columns = []
    for tile in range(tiles):
        piece = got[:, tile * chunk : (tile + 1) * chunk, :].astype(F32)
        columns.append(jnp.sum(piece * share, axis=0) / denominator)
    merged = jnp.concatenate(columns, axis=1)
    values = []
    first_copy.wait()
    for head in range(heads):
        rows = merged[ROWS * head : ROWS * (head + 1)].astype(BF16)
        values.append(jnp.dot(rows, value_in[head], preferred_element_type=F32))
    head_values = jnp.concatenate(values, axis=1).astype(BF16)
    span = keep.shape[2]
    for index, copy in enumerate(copies):
        copy.wait()
        attended = jnp.dot(
            head_values,
            project_in[:, index * step : (index + 1) * step],
            preferred_element_type=F32,
        )
        for inner in range(step // (2 * span)):
            even = attended[:, 2 * inner * span : (2 * inner + 1) * span]
            odd = attended[:, (2 * inner + 1) * span : (2 * inner + 2) * span]
            peer = index * step // (2 * span) + inner
            keep[peer] = jnp.where(core == 1, odd, even)
            send[peer] = jnp.where(core == 1, even, odd).astype(BF16)


def merge(got, value, project, span):
    peers = got.shape[0]
    depth, width = project.shape
    shape = (peers, ROWS, span)
    return pl.pallas_call(
        merge_kernel,
        out_shape=[jax.ShapeDtypeStruct(shape, F32), jax.ShapeDtypeStruct(shape, BF16)],
        in_specs=[VMEM] + [HBM] * 2,
        out_specs=[VMEM] * 2,
        scratch_shapes=[
            pltpu.VMEM(value.shape, BF16),
            pltpu.VMEM(project.shape, BF16),
            pltpu.SemaphoreType.DMA((5,)),
        ],
        compiler_params=params(16),
        cost_estimate=pl.CostEstimate(
            flops=2 * 8 * depth * width, bytes_accessed=6 * 2**20, transcendentals=0
        ),
        name="merge",
    )(got, *pinned(value, project))


def finish_kernel(keep, taken, mix, back_0, back_1, back_2, back_3, out):
    peers, _, span = keep.shape
    back = jnp.concatenate(
        [ref[...].astype(F32) for ref in (back_0, back_1, back_2, back_3)], axis=0
    ).astype(BF16)
    mixing = mix[...][:, : 4 * CAP]
    high = mixing.astype(BF16)
    low = (mixing - high.astype(F32)).astype(BF16)
    routed = jnp.dot(high, back, preferred_element_type=F32) + jnp.dot(
        low, back, preferred_element_type=F32
    )
    for peer in range(peers):
        attended = keep[peer] + taken[peer].astype(F32)
        both = jnp.concatenate([attended, routed[:, peer * span : (peer + 1) * span]], axis=0)
        out[peer] = both.astype(BF16)


def finish(keep, taken, mix, back):
    peers, rows, span = keep.shape
    return pl.pallas_call(
        finish_kernel,
        out_shape=jax.ShapeDtypeStruct((peers, 2 * rows, span), BF16),
        in_specs=[VMEM] * 7,
        out_specs=VMEM,
        compiler_params=params(8),
        name="finish",
    )(keep, taken, mix, *back)


def shards(
    query_lat,
    query_rope,
    cache_lat,
    cache_rope,
    lengths,
    w_value,
    w_out,
    moe_tokens,
    expert_ids,
    route_weights,
    w_gate,
    w_up,
    w_down,
):
    plane = ("y", "z")
    group_count = lax.axis_size("x")
    peers = lax.axis_size(plane)
    requests = cache_lat.shape[0]
    span = moe_tokens.shape[1]
    swap = [(0, 1), (1, 0)]

    def along_x(value, shift):
        return lax.ppermute(
            value, "x", [(i, (i + shift) % group_count) for i in range(group_count)]
        )

    query = lax.all_to_all(
        payload(query_lat, query_rope, moe_tokens, peers), plane, 0, 0, tiled=True
    )
    lat_far = lax.ppermute(cache_lat, "c", swap)
    rope_far = lax.ppermute(cache_rope, "c", swap)
    scale = (w_value.shape[2] + query_rope.shape[2]) ** (-0.5)
    part, *send, mix = attention(
        lengths,
        query,
        cache_lat,
        lat_far,
        cache_rope,
        rope_far,
        expert_ids,
        route_weights,
        scale,
        span,
        w_gate.shape[1],
    )
    got = lax.all_to_all(part, plane, 0, 0, tiled=True)

    near = [send[0]] + [along_x(send[d], d) for d in range(1, group_count)]
    own = jnp.concatenate(near, axis=0)
    far = lax.ppermute(own, "c", swap)
    keep, give = experts(own, far, w_gate, w_up, w_down)
    routed = pair(keep, lax.ppermute(give, "c", swap))
    back = [routed[0]] + [along_x(routed[d], -d) for d in range(1, group_count)]

    keep, give = merge(got, w_value, w_out, span)
    terms = finish(keep, lax.ppermute(give, "c", swap), mix, back)
    arrived = lax.all_to_all(terms, plane, 0, 0, tiled=True)
    summed = jnp.sum(arrived.astype(F32), axis=0).astype(BF16)
    return (summed[:requests], summed[requests:])


def solution(mesh):
    groups = mesh.shape["grp"]
    split = Mesh(mesh.devices.reshape(groups, 4, 8, 2), ("x",) + KV)
    both = ("x",) + KV
    return jax.shard_map(
        shards,
        mesh=split,
        in_specs=(
            P("x", KV, None),
            P("x", KV, None),
            P("x", KV, None),
            P("x", None, KV),
            P("x"),
            P(KV, None, None),
            P(KV, None),
            P("x", KV),
            P("x", None),
            P("x", None),
            P(None, both),
            P(None, both),
            P(both, None),
        ),
        out_specs=(P("x", KV), P("x", KV)),
        check_vma=False,
    )
```

```python
import jax
import jax.numpy as jnp
from jax import lax
from jax.experimental import pallas as pl
from jax.experimental.pallas import tpu as pltpu
from jax.sharding import Mesh
from jax.sharding import PartitionSpec as P

FF = 1024
CAP = 4
ROWS = 8
F32 = jnp.float32
BF16 = jnp.bfloat16
LANES = 128
KV = ("y", "z", "c")
VMEM = pl.BlockSpec(memory_space=pltpu.VMEM)
SMEM = pl.BlockSpec(memory_space=pltpu.SMEM)
ANY = pl.BlockSpec(memory_space=pl.ANY)
HBM = pl.BlockSpec(memory_space=pltpu.HBM)


def three_terms(value):
    high = value.astype(BF16).astype(F32)
    rest = value - high
    middle = rest.astype(BF16).astype(F32)
    return high, middle, rest - middle


def pinned(*values):
    return [pltpu.with_memory_space_constraint(value, pltpu.HBM) for value in values]


def params(mebibytes):
    return pltpu.CompilerParams(vmem_limit_bytes=mebibytes * 2**20)


def fetch_kernel(after, *refs):
    del after
    count = len(refs) // 2
    sems = refs[-1]
    copies = [
        pltpu.make_async_copy(refs[index], refs[count + index], sems.at[index])
        for index in range(count)
    ]
    for copy in copies:
        copy.start()
    for copy in copies:
        copy.wait()


def fetch(after, *values):
    moved = sum(value.size * value.dtype.itemsize for value in values)
    return pl.pallas_call(
        fetch_kernel,
        out_shape=[pltpu.VMEM(value.shape, value.dtype) for value in values],
        in_specs=[ANY] + [HBM] * len(values),
        out_specs=[VMEM] * len(values),
        scratch_shapes=[pltpu.SemaphoreType.DMA((len(values),))],
        compiler_params=params(1),
        cost_estimate=pl.CostEstimate(flops=0, bytes_accessed=moved, transcendentals=0),
        name="fetch",
    )(after, *pinned(*values))


def payload_kernel(query_lat, query_rope, tokens, out, lat_in, rope_in, tokens_in, sems):
    copies = [
        pltpu.make_async_copy(source, target, sems.at[index])
        for index, (source, target) in enumerate(
            ((query_lat, lat_in), (query_rope, rope_in), (tokens, tokens_in))
        )
    ]
    for copy in copies:
        copy.start()
    for copy in copies:
        copy.wait()
    peers = out.shape[0]
    latent, rope = query_lat.shape[2], query_rope.shape[2]
    heads = query_lat.shape[1]
    half = tokens.shape[1] // heads
    lat = lat_in[...].astype(F32)
    rot = rope_in[...].astype(F32)
    tok = tokens_in[...].astype(F32)
    spare = jnp.zeros((ROWS, out.shape[2] - latent - rope - half), F32)
    rows = []
    for head in range(heads):
        tail = jnp.concatenate(
            [rot[:, head, :], tok[:, head * half : (head + 1) * half], spare], axis=1
        )
        rows.append(jnp.concatenate([lat[:, head, :], tail], axis=1))
    chunk = jnp.concatenate(rows, axis=0).astype(BF16)
    for peer in range(peers):
        out[peer] = chunk


def payload(query_lat, query_rope, tokens, peers):
    requests, heads, latent = query_lat.shape
    return pl.pallas_call(
        payload_kernel,
        out_shape=jax.ShapeDtypeStruct((peers, heads * requests, latent + LANES), BF16),
        in_specs=[HBM] * 3,
        out_specs=VMEM,
        scratch_shapes=[
            pltpu.VMEM(query_lat.shape, BF16),
            pltpu.VMEM(query_rope.shape, BF16),
            pltpu.VMEM(tokens.shape, BF16),
            pltpu.SemaphoreType.DMA((3,)),
        ],
        compiler_params=params(20),
        name="payload",
    )(*pinned(query_lat, query_rope, tokens))


def attention_kernel(
    lengths,
    query,
    lat_own,
    lat_far,
    rope_own,
    rope_far,
    ids,
    route,
    out,
    send_0,
    send_1,
    send_2,
    send_3,
    mix_out,
    query_rows,
    out_rows,
    stat_rows,
    token_rows,
    lengths_in,
    ids_in,
    route_in,
    sems,
    *,
    scale,
    units,
):
    peers, chunk, width = query.shape
    requests, positions, latent = lat_own.shape
    small = [
        pltpu.make_async_copy(lengths, lengths_in, sems.at[0]),
        pltpu.make_async_copy(ids, ids_in, sems.at[1]),
        pltpu.make_async_copy(route, route_in, sems.at[2]),
    ]
    for copy in small:
        copy.start()
    rope = rope_own.shape[1]
    tiles = latent // LANES
    heads = chunk // requests
    group, groups = lax.axis_index("x"), lax.axis_size("x")
    shard, shards_here = lax.axis_index(KV), lax.axis_size(KV)
    core = lax.axis_index("c")
    rows = peers * heads

    for tile in range(tiles + 1):
        piece = query[:, :, tile * LANES : (tile + 1) * LANES].astype(F32)
        query_rows[tile] = piece.reshape(peers * chunk, LANES)

    half = token_rows.shape[1] // (peers * heads)
    for peer in range(peers):
        begin = peer * chunk
        pieces = [
            query_rows[tiles, begin + requests * head : begin + requests * (head + 1), :][
                :, rope : rope + half
            ]
            for head in range(heads)
        ]
        token_rows[:, peer * heads * half : (peer + 1) * heads * half] = jnp.concatenate(
            pieces, axis=1
        )
    tokens = token_rows[...].astype(BF16)
    for copy in small:
        copy.wait()
    named = ids_in[...]
    strength = route_in[...]
    lower = (
        lax.broadcasted_iota(jnp.int32, (ROWS, ROWS), 1)
        < lax.broadcasted_iota(jnp.int32, (ROWS, ROWS), 0)
    ).astype(F32)
    slot_lane = lax.broadcasted_iota(jnp.int32, (ROWS, LANES), 1)
    placing = jnp.zeros((ROWS, LANES), F32)
    mix = jnp.zeros((ROWS, LANES), F32)
    for step in range(4):
        expert = (lax.rem(group + step, groups) * shards_here + shard) * units // FF
        hit = named == expert
        chosen = jnp.max(jnp.where(hit, 1.0, 0.0), axis=1, keepdims=True)
        weight = jnp.sum(jnp.where(hit, strength, 0.0), axis=1, keepdims=True)
        chosen_wide = jnp.broadcast_to(chosen, (ROWS, LANES))
        rank = jnp.dot(lower, chosen_wide, preferred_element_type=F32)
        picked = (rank == (slot_lane - CAP * step).astype(F32)) & (chosen_wide > 0.0)
        picked = picked & (slot_lane >= CAP * step) & (slot_lane < CAP * (step + 1))
        placing = jnp.where(picked, 1.0, placing)
        mix = jnp.where(picked, weight, mix)
    mix_out[...] = mix
    select = placing.T[: 4 * CAP, :].astype(BF16)
    chosen_rows = jnp.dot(select, tokens, preferred_element_type=F32).astype(BF16)
    for step, send in enumerate((send_0, send_1, send_2, send_3)):
        send[...] = chosen_rows[CAP * step : CAP * (step + 1)]

    lane = lax.broadcasted_iota(jnp.int32, (rows, LANES), 1)
    stats = jnp.zeros((rows, LANES), F32)
    base_own = shard * positions
    base_far = (shard + 1 - 2 * core) * positions
    place = lax.broadcasted_iota(jnp.int32, (rows, positions), 1)
    for request in range(requests):
        mine = jnp.concatenate(
            [
                jnp.concatenate(
                    [
                        query_rows[tile, pl.ds(requests * head + request, peers, stride=chunk), :]
                        for tile in range(tiles + 1)
                    ],
                    axis=1,
                )
                for head in range(heads)
            ],
            axis=0,
        ).astype(BF16)
        length = lengths_in[request]
        parts = []
        for lat, rot, base in ((lat_own, rope_own, base_own), (lat_far, rope_far, base_far)):
            score = (
                lax.dot_general(
                    mine[:, :latent],
                    lat[request],
                    (((1,), (1,)), ((), ())),
                    preferred_element_type=F32,
                )
                + jnp.dot(
                    mine[:, latent : latent + rope], rot[request], preferred_element_type=F32
                )
            ) * scale
            usable = place < length - base
            parts.append((jnp.where(usable, score, -1e30), usable, lat))
        top = jnp.max(jnp.maximum(parts[0][0], parts[1][0]), axis=1, keepdims=True)
        weights = [jnp.where(usable, jnp.exp(score - top), 0.0) for score, usable, _ in parts]
        total = jnp.sum(weights[0] + weights[1], axis=1, keepdims=True)
        weighted = jnp.dot(
            weights[0].astype(BF16), lat_own[request], preferred_element_type=F32
        ) + jnp.dot(weights[1].astype(BF16), lat_far[request], preferred_element_type=F32)
        partial = weighted * (1.0 / jnp.maximum(total, 1.0))
        for index, term in enumerate(three_terms(top) + three_terms(total)):
            stats = jnp.where(lane == ROWS * request + index, term, stats)
        for head in range(heads):
            for tile in range(tiles):
                out_rows[tile, pl.ds(requests * head + request, peers, stride=chunk), :] = partial[
                    peers * head : peers * (head + 1), tile * LANES : (tile + 1) * LANES
                ]

    for tile in range(tiles):
        out[:, tile * chunk : (tile + 1) * chunk, :] = (
            out_rows[tile].reshape(peers, chunk, LANES).astype(BF16)
        )
    stat_rows[...] = jnp.zeros_like(stat_rows)
    for head in range(heads):
        stat_rows[pl.ds(head, peers, stride=ROWS), :] = stats[peers * head : peers * (head + 1)]
    out[:, tiles * chunk :, :] = stat_rows[...].reshape(peers, ROWS, LANES).astype(BF16)


def attention(lengths, query, lat_own, lat_far, rope_own, rope_far, ids, route, scale, span, units):
    peers, chunk, width = query.shape
    requests, positions, latent = lat_own.shape
    rope = rope_own.shape[1]
    tiles = latent // LANES
    lengths, ids, route = pinned(lengths, ids, route)
    return pl.pallas_call(
        lambda *refs: attention_kernel(*refs, scale=scale, units=units),
        out_shape=[jax.ShapeDtypeStruct((peers, tiles * chunk + ROWS, LANES), BF16)]
        + [jax.ShapeDtypeStruct((CAP, peers * span), BF16)] * 4
        + [jax.ShapeDtypeStruct((ROWS, LANES), F32)],
        in_specs=[HBM] + [VMEM] * 5 + [HBM] * 2,
        out_specs=[VMEM] * 6,
        scratch_shapes=[
            pltpu.VMEM((width // LANES, peers * chunk, LANES), F32),
            pltpu.VMEM((tiles, peers * chunk, LANES), F32),
            pltpu.VMEM((peers * ROWS, LANES), F32),
            pltpu.VMEM((requests, peers * span), F32),
            pltpu.SMEM(lengths.shape, jnp.int32),
            pltpu.VMEM(ids.shape, jnp.int32),
            pltpu.VMEM(route.shape, F32),
            pltpu.SemaphoreType.DMA((3,)),
        ],
        compiler_params=params(24),
        cost_estimate=pl.CostEstimate(
            flops=2 * peers * chunk * 2 * positions * (2 * latent + rope),
            bytes_accessed=6 * 2**20,
            transcendentals=peers * chunk * 2 * positions,
        ),
        name="attention",
    )(lengths, query, lat_own, lat_far, rope_own, rope_far, ids, route)


def stack_kernel(after, *refs):
    del after
    out = refs[-1]
    out[...] = jnp.concatenate([ref[...].astype(F32) for ref in refs[:-1]], axis=0).astype(BF16)


def stack(after, *values):
    rows, width = values[0].shape
    return pl.pallas_call(
        stack_kernel,
        out_shape=jax.ShapeDtypeStruct((len(values) * rows, width), BF16),
        in_specs=[ANY] + [VMEM] * len(values),
        out_specs=VMEM,
        compiler_params=params(4),
        name="stack",
    )(after, *values)


def experts_kernel(own, far, gate, up, down, keep, send):
    depth, units = gate.shape
    width = down.shape[1]
    span = 112
    blocks = depth // (2 * span)
    core = lax.axis_index("c")
    each = 8
    total = jnp.zeros((own.shape[0], 2 * units), F32)
    for index in range(blocks // each):
        for tokens, parity in ((own, core), (far, 1 - core)):
            columns = []
            for source in (gate, up):
                columns.append(
                    jnp.concatenate(
                        [
                            source[
                                pl.ds(
                                    pl.multiple_of(2 * span * block + span * parity, 16), span
                                ),
                                :,
                            ]
                            for block in range(each * index, each * (index + 1))
                        ],
                        axis=0,
                    )
                )
            total += jnp.dot(
                tokens[:, each * span * index : each * span * (index + 1)],
                jnp.concatenate(columns, axis=1),
                preferred_element_type=F32,
            )
    gate_proj, up_proj = total[:, :units], total[:, units:]
    hidden = (gate_proj * jax.nn.sigmoid(gate_proj) * up_proj).astype(BF16)
    pair = 2 * span
    step = 8 * span
    for start in range(0, width, step):
        result = jnp.dot(hidden, down[:, start : start + step], preferred_element_type=F32)
        evens, odds = [], []
        for inner in range(0, step, pair):
            evens.append(result[:, inner : inner + span])
            odds.append(result[:, inner + span : inner + pair])
        even, odd = jnp.concatenate(evens, axis=1), jnp.concatenate(odds, axis=1)
        here = slice(start // 2, (start + step) // 2)
        keep[:, here] = jnp.where(core == 1, odd, even)
        send[:, here] = jnp.where(core == 1, even, odd).astype(BF16)


def experts(own, far, gate, up, down):
    depth, units = gate.shape
    width = down.shape[1]
    shape = (own.shape[0], width // 2)
    return pl.pallas_call(
        experts_kernel,
        out_shape=[jax.ShapeDtypeStruct(shape, F32), jax.ShapeDtypeStruct(shape, BF16)],
        in_specs=[VMEM] * 5,
        out_specs=[VMEM] * 2,
        compiler_params=params(16),
        cost_estimate=pl.CostEstimate(
            flops=2 * 16 * 3 * depth * units, bytes_accessed=6 * 2**20, transcendentals=0
        ),
        name="experts",
    )(own, far, gate, up, down)


def pair_kernel(keep, taken, *outs):
    total = (keep[...] + taken[...].astype(F32)).astype(BF16)
    for block, out in enumerate(outs):
        out[...] = total[CAP * block : CAP * (block + 1)]


def pair(keep, taken):
    width = keep.shape[1]
    return pl.pallas_call(
        pair_kernel,
        out_shape=[jax.ShapeDtypeStruct((CAP, width), BF16)] * 4,
        in_specs=[VMEM] * 2,
        out_specs=[VMEM] * 4,
        compiler_params=params(8),
        name="pair",
    )(keep, taken)


def merge_kernel(after, got, value, out):
    del after
    peers, height, _ = got.shape
    heads = value.shape[0]
    chunk = ROWS * heads
    tiles = height // chunk
    stats = got[:, tiles * chunk :, :].astype(F32)
    lane = lax.broadcasted_iota(jnp.int32, (peers, ROWS, LANES), 2)
    first = lane - ROWS * lax.broadcasted_iota(jnp.int32, (peers, ROWS, LANES), 1)
    tops, totals = [], []
    for head in range(heads):
        row = jnp.broadcast_to(stats[:, head : head + 1, :], (peers, ROWS, LANES))
        tops.append(
            jnp.sum(jnp.where((first >= 0) & (first < 3), row, 0.0), axis=2, keepdims=True)
        )
        totals.append(
            jnp.sum(jnp.where((first >= 3) & (first < 6), row, 0.0), axis=2, keepdims=True)
        )
    top = jnp.concatenate(tops, axis=1)
    total = jnp.concatenate(totals, axis=1)
    peak = jnp.max(top, axis=0, keepdims=True)
    share = total * jnp.exp(top - peak)
    denominator = jnp.sum(share, axis=0)
    columns = []
    for tile in range(tiles):
        piece = got[:, tile * chunk : (tile + 1) * chunk, :].astype(F32)
        columns.append(jnp.sum(piece * share, axis=0) / denominator)
    merged = jnp.concatenate(columns, axis=1)
    values = []
    for head in range(heads):
        rows = merged[ROWS * head : ROWS * (head + 1)].astype(BF16)
        values.append(jnp.dot(rows, value[head], preferred_element_type=F32))
    out[...] = jnp.concatenate(values, axis=1).astype(BF16)


def merge(after, got, value):
    heads, latent, width = value.shape
    return pl.pallas_call(
        merge_kernel,
        out_shape=jax.ShapeDtypeStruct((ROWS, heads * width), BF16),
        in_specs=[ANY] + [VMEM] * 2,
        out_specs=VMEM,
        compiler_params=params(16),
        cost_estimate=pl.CostEstimate(
            flops=2 * ROWS * heads * latent * width, bytes_accessed=2**20, transcendentals=0
        ),
        name="merge",
    )(after, got, value)


def finish_kernel(
    values, values_far, project, project_far, mix, back_0, back_1, back_2, back_3, out
):
    peers, _, span = out.shape
    back = jnp.concatenate(
        [ref[...].astype(F32) for ref in (back_0, back_1, back_2, back_3)], axis=0
    ).astype(BF16)
    mixing = mix[...][:, : 4 * CAP]
    high = mixing.astype(BF16)
    low = (mixing - high.astype(F32)).astype(BF16)
    step = 8 * span
    for start in range(0, peers * span, step):
        here = slice(start, start + step)
        routed = jnp.dot(high, back[:, here], preferred_element_type=F32) + jnp.dot(
            low, back[:, here], preferred_element_type=F32
        )
        attended = jnp.dot(
            values[...], project[:, here], preferred_element_type=F32
        ) + jnp.dot(values_far[...], project_far[:, here], preferred_element_type=F32)
        both = jnp.concatenate([attended, routed], axis=0)
        for inner in range(8):
            out[start // span + inner] = both[:, inner * span : (inner + 1) * span].astype(BF16)


def finish(values, values_far, project, project_far, mix, back, peers, span):
    return pl.pallas_call(
        finish_kernel,
        out_shape=jax.ShapeDtypeStruct((peers, 2 * ROWS, span), BF16),
        in_specs=[VMEM] * 9,
        out_specs=VMEM,
        compiler_params=params(16),
        name="finish",
    )(values, values_far, project, project_far, mix, *back)


def split_kernel(after, project, mine, theirs):
    del after
    span = 112
    step = 8 * span
    core = lax.axis_index("c")

    @pl.loop(0, project.shape[0] // 32)
    def _(block):
        rows = pl.ds(pl.multiple_of(block * 32, 32), 32)
        for start in range(0, project.shape[1], 2 * step):
            piece = project[rows, start : start + 2 * step].astype(F32)
            even = jnp.concatenate(
                [piece[:, 2 * i * span : (2 * i + 1) * span] for i in range(8)], axis=1
            )
            odd = jnp.concatenate(
                [piece[:, (2 * i + 1) * span : (2 * i + 2) * span] for i in range(8)], axis=1
            )
            here = slice(start // 2, start // 2 + step)
            mine[rows, here] = jnp.where(core == 1, odd, even).astype(BF16)
            theirs[rows, here] = jnp.where(core == 1, even, odd).astype(BF16)


def split(after, project):
    depth, width = project.shape
    return pl.pallas_call(
        split_kernel,
        out_shape=[pltpu.HBM((depth, width // 2), BF16)] * 2,
        in_specs=[ANY, VMEM],
        out_specs=[VMEM] * 2,
        compiler_params=params(20),
        cost_estimate=pl.CostEstimate(flops=0, bytes_accessed=8 * 2**20, transcendentals=0),
        name="split",
    )(after, *pinned(project))


def shards(
    query_lat,
    query_rope,
    cache_lat,
    cache_rope,
    lengths,
    w_value,
    w_out,
    moe_tokens,
    expert_ids,
    route_weights,
    w_gate,
    w_up,
    w_down,
):
    plane = ("y", "z")
    group_count = lax.axis_size("x")
    peers = lax.axis_size(plane)
    requests = cache_lat.shape[0]
    span = moe_tokens.shape[1]
    swap = [(0, 1), (1, 0)]

    def along_x(value, shift):
        return lax.ppermute(
            value, "x", [(i, (i + shift) % group_count) for i in range(group_count)]
        )

    query = lax.all_to_all(
        payload(query_lat, query_rope, moe_tokens, peers), plane, 0, 0, tiled=True
    )
    lat_far = lax.ppermute(cache_lat, "c", swap)
    rope_far = lax.ppermute(cache_rope, "c", swap)
    project, theirs = split(rope_far, w_out)
    project_far = lax.ppermute(theirs, "c", swap)
    lat_own, rope_own = fetch(rope_far, cache_lat, cache_rope)
    scale = (w_value.shape[2] + query_rope.shape[2]) ** (-0.5)
    part, *send, mix = attention(
        lengths,
        query,
        lat_own,
        lat_far,
        rope_own,
        rope_far,
        expert_ids,
        route_weights,
        scale,
        span,
        w_gate.shape[1],
    )
    got = lax.all_to_all(part, plane, 0, 0, tiled=True)

    near = [send[0]] + [along_x(send[d], d) for d in range(1, group_count)]
    gate, up, down = fetch(part, w_gate, w_up, w_down)
    own = stack(gate, *near)
    far = lax.ppermute(own, "c", swap)
    keep, give = experts(own, far, gate, up, down)
    routed = pair(keep, lax.ppermute(give, "c", swap))
    back = [routed[0]] + [along_x(routed[d], -d) for d in range(1, group_count)]

    project, value = fetch(routed[0], project, w_value)
    values = merge(routed[0], got, value)
    values_far = lax.ppermute(values, "c", swap)
    terms = finish(values, values_far, project, project_far, mix, back, peers, span)
    arrived = lax.all_to_all(terms, plane, 0, 0, tiled=True)
    summed = jnp.sum(arrived.astype(F32), axis=0).astype(BF16)
    return (summed[:requests], summed[requests:])


def solution(mesh):
    groups = mesh.shape["grp"]
    split = Mesh(mesh.devices.reshape(groups, 4, 8, 2), ("x",) + KV)
    both = ("x",) + KV
    return jax.shard_map(
        shards,
        mesh=split,
        in_specs=(
            P("x", KV, None),
            P("x", KV, None),
            P("x", KV, None),
            P("x", None, KV),
            P("x"),
            P(KV, None, None),
            P(KV, None),
            P("x", KV),
            P("x", None),
            P("x", None),
            P(None, both),
            P(None, both),
            P(both, None),
        ),
        out_specs=(P("x", KV), P("x", KV)),
        check_vma=False,
    )
```

```python
import jax
import jax.numpy as jnp
from jax import lax
from jax.experimental import pallas as pl
from jax.experimental.pallas import tpu as pltpu
from jax.sharding import Mesh
from jax.sharding import PartitionSpec as P

FF = 1024
CAP = 4
ROWS = 8
F32 = jnp.float32
BF16 = jnp.bfloat16
LANES = 128
KV = ("y", "z", "c")
VMEM = pl.BlockSpec(memory_space=pltpu.VMEM)
SMEM = pl.BlockSpec(memory_space=pltpu.SMEM)
ANY = pl.BlockSpec(memory_space=pl.ANY)
HBM = pl.BlockSpec(memory_space=pltpu.HBM)


def three_terms(value):
    high = value.astype(BF16).astype(F32)
    rest = value - high
    middle = rest.astype(BF16).astype(F32)
    return high, middle, rest - middle


def pinned(*values):
    return [pltpu.with_memory_space_constraint(value, pltpu.HBM) for value in values]


def params(mebibytes):
    return pltpu.CompilerParams(vmem_limit_bytes=mebibytes * 2**20)


def fetch_kernel(after, *refs):
    del after
    count = len(refs) // 2
    sems = refs[-1]
    copies = [
        pltpu.make_async_copy(refs[index], refs[count + index], sems.at[index])
        for index in range(count)
    ]
    for copy in copies:
        copy.start()
    for copy in copies:
        copy.wait()


def fetch(after, *values):
    moved = sum(value.size * value.dtype.itemsize for value in values)
    return pl.pallas_call(
        fetch_kernel,
        out_shape=[pltpu.VMEM(value.shape, value.dtype) for value in values],
        in_specs=[ANY] + [HBM] * len(values),
        out_specs=[VMEM] * len(values),
        scratch_shapes=[pltpu.SemaphoreType.DMA((len(values),))],
        compiler_params=params(1),
        cost_estimate=pl.CostEstimate(flops=0, bytes_accessed=moved, transcendentals=0),
        name="fetch",
    )(after, *pinned(*values))


def payload_kernel(query_lat, query_rope, tokens, out, lat_in, rope_in, tokens_in, sems):
    copies = [
        pltpu.make_async_copy(source, target, sems.at[index])
        for index, (source, target) in enumerate(
            ((query_lat, lat_in), (query_rope, rope_in), (tokens, tokens_in))
        )
    ]
    for copy in copies:
        copy.start()
    for copy in copies:
        copy.wait()
    peers = out.shape[0]
    latent, rope = query_lat.shape[2], query_rope.shape[2]
    heads = query_lat.shape[1]
    half = tokens.shape[1] // heads
    lat = lat_in[...].astype(F32)
    rot = rope_in[...].astype(F32)
    tok = tokens_in[...].astype(F32)
    spare = jnp.zeros((ROWS, out.shape[2] - latent - rope - half), F32)
    rows = []
    for head in range(heads):
        tail = jnp.concatenate(
            [rot[:, head, :], tok[:, head * half : (head + 1) * half], spare], axis=1
        )
        rows.append(jnp.concatenate([lat[:, head, :], tail], axis=1))
    chunk = jnp.concatenate(rows, axis=0).astype(BF16)
    for peer in range(peers):
        out[peer] = chunk


def payload(query_lat, query_rope, tokens, peers):
    requests, heads, latent = query_lat.shape
    return pl.pallas_call(
        payload_kernel,
        out_shape=jax.ShapeDtypeStruct((peers, heads * requests, latent + LANES), BF16),
        in_specs=[HBM] * 3,
        out_specs=VMEM,
        scratch_shapes=[
            pltpu.VMEM(query_lat.shape, BF16),
            pltpu.VMEM(query_rope.shape, BF16),
            pltpu.VMEM(tokens.shape, BF16),
            pltpu.SemaphoreType.DMA((3,)),
        ],
        compiler_params=params(20),
        name="payload",
    )(*pinned(query_lat, query_rope, tokens))


def attention_kernel(
    lengths,
    query,
    query_one,
    query_two,
    query_three,
    lat_own,
    lat_far,
    rope_own,
    rope_far,
    ids,
    route,
    out,
    send_0,
    send_1,
    send_2,
    send_3,
    mix_out,
    query_rows,
    out_rows,
    stat_rows,
    token_rows,
    lengths_in,
    lat_in,
    rope_in,
    ids_in,
    route_in,
    sems,
    *,
    scale,
    units,
):
    ring, chunk, width = query.shape
    peers = 4 * ring
    requests, positions, latent = lat_own.shape
    small = [
        pltpu.make_async_copy(lengths, lengths_in, sems.at[0]),
        pltpu.make_async_copy(ids, ids_in, sems.at[1]),
        pltpu.make_async_copy(route, route_in, sems.at[2]),
    ]
    large = [
        pltpu.make_async_copy(rope_own, rope_in, sems.at[3]),
    ] + [
        pltpu.make_async_copy(
            lat_own.at[pl.ds(half_of, requests // 2)],
            lat_in.at[pl.ds(half_of, requests // 2)],
            sems.at[4 + half_of // (requests // 2)],
        )
        for half_of in range(0, requests, requests // 2)
    ]
    for copy in small + large:
        copy.start()
    rope = rope_own.shape[1]
    tiles = latent // LANES
    heads = chunk // requests
    group, groups = lax.axis_index("x"), lax.axis_size("x")
    shard, shards_here = lax.axis_index(KV), lax.axis_size(KV)
    core = lax.axis_index("c")
    rows = peers * heads

    row = lax.axis_index("y")
    for step, source in enumerate((query, query_one, query_two, query_three)):
        begin = pl.multiple_of(lax.rem(row + 4 - step, 4) * (ring * chunk), ring * chunk)
        for tile in range(tiles + 1):
            piece = source[:, :, tile * LANES : (tile + 1) * LANES].astype(F32)
            query_rows[tile, pl.ds(begin, ring * chunk), :] = piece.reshape(ring * chunk, LANES)

    half = token_rows.shape[1] // (peers * heads)
    for peer in range(peers):
        begin = peer * chunk
        pieces = [
            query_rows[tiles, begin + requests * head : begin + requests * (head + 1), :][
                :, rope : rope + half
            ]
            for head in range(heads)
        ]
        token_rows[:, peer * heads * half : (peer + 1) * heads * half] = jnp.concatenate(
            pieces, axis=1
        )
    tokens = token_rows[...].astype(BF16)
    for copy in small:
        copy.wait()
    named = ids_in[...]
    strength = route_in[...]
    lower = (
        lax.broadcasted_iota(jnp.int32, (ROWS, ROWS), 1)
        < lax.broadcasted_iota(jnp.int32, (ROWS, ROWS), 0)
    ).astype(F32)
    slot_lane = lax.broadcasted_iota(jnp.int32, (ROWS, LANES), 1)
    placing = jnp.zeros((ROWS, LANES), F32)
    mix = jnp.zeros((ROWS, LANES), F32)
    for step in range(4):
        expert = (lax.rem(group + step, groups) * shards_here + shard) * units // FF
        hit = named == expert
        chosen = jnp.max(jnp.where(hit, 1.0, 0.0), axis=1, keepdims=True)
        weight = jnp.sum(jnp.where(hit, strength, 0.0), axis=1, keepdims=True)
        chosen_wide = jnp.broadcast_to(chosen, (ROWS, LANES))
        rank = jnp.dot(lower, chosen_wide, preferred_element_type=F32)
        picked = (rank == (slot_lane - CAP * step).astype(F32)) & (chosen_wide > 0.0)
        picked = picked & (slot_lane >= CAP * step) & (slot_lane < CAP * (step + 1))
        placing = jnp.where(picked, 1.0, placing)
        mix = jnp.where(picked, weight, mix)
    mix_out[...] = mix
    select = placing.T[: 4 * CAP, :].astype(BF16)
    chosen_rows = jnp.dot(select, tokens, preferred_element_type=F32).astype(BF16)
    for step, send in enumerate((send_0, send_1, send_2, send_3)):
        send[...] = chosen_rows[CAP * step : CAP * (step + 1)]

    lane = lax.broadcasted_iota(jnp.int32, (rows, LANES), 1)
    stats = jnp.zeros((rows, LANES), F32)
    base_own = shard * positions
    base_far = (shard + 1 - 2 * core) * positions
    place = lax.broadcasted_iota(jnp.int32, (rows, positions), 1)
    queries = []
    for request in range(requests):
        queries.append(
            jnp.concatenate(
                [
                    jnp.concatenate(
                        [
                            query_rows[
                                tile, pl.ds(requests * head + request, peers, stride=chunk), :
                            ]
                            for tile in range(tiles + 1)
                        ],
                        axis=1,
                    )
                    for head in range(heads)
                ],
                axis=0,
            ).astype(BF16)
        )

    def scores(request, lat, rot, base):
        mine = queries[request]
        score = (
            lax.dot_general(
                mine[:, :latent],
                lat[request],
                (((1,), (1,)), ((), ())),
                preferred_element_type=F32,
            )
            + jnp.dot(mine[:, latent : latent + rope], rot[request], preferred_element_type=F32)
        ) * scale
        usable = place < lengths_in[request] - base
        return jnp.where(usable, score, -1e30), usable

    for request in range(requests):
        if request == 0:
            large[0].wait()
            large[1].wait()
        if request == requests // 2:
            large[2].wait()
        parts = [
            scores(request, lat_in, rope_in, base_own),
            scores(request, lat_far, rope_far, base_far),
        ]
        top = jnp.max(jnp.maximum(parts[0][0], parts[1][0]), axis=1, keepdims=True)
        weights = [jnp.where(usable, jnp.exp(score - top), 0.0) for score, usable in parts]
        total = jnp.sum(weights[0] + weights[1], axis=1, keepdims=True)
        weighted = jnp.dot(
            weights[0].astype(BF16), lat_in[request], preferred_element_type=F32
        ) + jnp.dot(weights[1].astype(BF16), lat_far[request], preferred_element_type=F32)
        partial = weighted * (1.0 / jnp.maximum(total, 1.0))
        for index, term in enumerate(three_terms(top) + three_terms(total)):
            stats = jnp.where(lane == ROWS * request + index, term, stats)
        for head in range(heads):
            for tile in range(tiles):
                out_rows[tile, pl.ds(requests * head + request, peers, stride=chunk), :] = partial[
                    peers * head : peers * (head + 1), tile * LANES : (tile + 1) * LANES
                ]

    for tile in range(tiles):
        out[:, tile * chunk : (tile + 1) * chunk, :] = (
            out_rows[tile].reshape(peers, chunk, LANES).astype(BF16)
        )
    stat_rows[...] = jnp.zeros_like(stat_rows)
    for head in range(heads):
        stat_rows[pl.ds(head, peers, stride=ROWS), :] = stats[peers * head : peers * (head + 1)]
    out[:, tiles * chunk :, :] = stat_rows[...].reshape(peers, ROWS, LANES).astype(BF16)


def attention(lengths, query, lat_own, lat_far, rope_own, rope_far, ids, route, scale, span, units):
    peers, chunk, width = 4 * query[0].shape[0], *query[0].shape[1:]
    requests, positions, latent = lat_own.shape
    rope = rope_own.shape[1]
    tiles = latent // LANES
    lengths, lat_own, rope_own, ids, route = pinned(lengths, lat_own, rope_own, ids, route)
    return pl.pallas_call(
        lambda *refs: attention_kernel(*refs, scale=scale, units=units),
        out_shape=[jax.ShapeDtypeStruct((peers, tiles * chunk + ROWS, LANES), BF16)]
        + [jax.ShapeDtypeStruct((CAP, peers * span), BF16)] * 4
        + [jax.ShapeDtypeStruct((ROWS, LANES), F32)],
        in_specs=[HBM] + [VMEM] * 4 + [HBM, VMEM, HBM, VMEM, HBM, HBM],
        out_specs=[VMEM] * 6,
        scratch_shapes=[
            pltpu.VMEM((width // LANES, peers * chunk, LANES), F32),
            pltpu.VMEM((tiles, peers * chunk, LANES), F32),
            pltpu.VMEM((peers * ROWS, LANES), F32),
            pltpu.VMEM((requests, peers * span), F32),
            pltpu.SMEM(lengths.shape, jnp.int32),
            pltpu.VMEM(lat_own.shape, BF16),
            pltpu.VMEM(rope_own.shape, BF16),
            pltpu.VMEM(ids.shape, jnp.int32),
            pltpu.VMEM(route.shape, F32),
            pltpu.SemaphoreType.DMA((6,)),
        ],
        compiler_params=params(24),
        cost_estimate=pl.CostEstimate(
            flops=2 * peers * chunk * 2 * positions * (2 * latent + rope),
            bytes_accessed=6 * 2**20,
            transcendentals=peers * chunk * 2 * positions,
        ),
        name="attention",
    )(lengths, *query, lat_own, lat_far, rope_own, rope_far, ids, route)


def stack_kernel(after, *refs):
    del after
    out = refs[-1]
    out[...] = jnp.concatenate([ref[...].astype(F32) for ref in refs[:-1]], axis=0).astype(BF16)


def stack(after, *values):
    rows, width = values[0].shape
    return pl.pallas_call(
        stack_kernel,
        out_shape=jax.ShapeDtypeStruct((len(values) * rows, width), BF16),
        in_specs=[ANY] + [VMEM] * len(values),
        out_specs=VMEM,
        compiler_params=params(4),
        name="stack",
    )(after, *values)


def experts_kernel(own, far, gate, up, down, *outs):
    depth, units = gate.shape
    width = down.shape[1]
    span = 112
    blocks = depth // (2 * span)
    core = lax.axis_index("c")
    each = 8
    total = jnp.zeros((own.shape[0], 2 * units), F32)
    for index in range(blocks // each):
        for tokens, parity in ((own, core), (far, 1 - core)):
            columns = []
            for source in (gate, up):
                columns.append(
                    jnp.concatenate(
                        [
                            source[
                                pl.ds(
                                    pl.multiple_of(2 * span * block + span * parity, 16), span
                                ),
                                :,
                            ]
                            for block in range(each * index, each * (index + 1))
                        ],
                        axis=0,
                    )
                )
            total += jnp.dot(
                tokens[:, each * span * index : each * span * (index + 1)],
                jnp.concatenate(columns, axis=1),
                preferred_element_type=F32,
            )
    gate_proj, up_proj = total[:, :units], total[:, units:]
    hidden = (gate_proj * jax.nn.sigmoid(gate_proj) * up_proj).astype(BF16)
    step = 1024
    for start in range(0, width, step):
        here = slice(start, start + step)
        result = jnp.dot(hidden, down[:, here], preferred_element_type=F32).astype(BF16)
        for block, out in enumerate(outs):
            out[:, here] = result[CAP * block : CAP * (block + 1)]


def experts(own, far, gate, up, down):
    depth, units = gate.shape
    width = down.shape[1]
    return pl.pallas_call(
        experts_kernel,
        out_shape=[jax.ShapeDtypeStruct((CAP, width), BF16)] * 4,
        in_specs=[VMEM] * 5,
        out_specs=[VMEM] * 4,
        compiler_params=params(16),
        cost_estimate=pl.CostEstimate(
            flops=2 * 16 * 3 * depth * units, bytes_accessed=6 * 2**20, transcendentals=0
        ),
        name="experts",
    )(own, far, gate, up, down)


def merge_kernel(after, got, value, project, out, value_in, project_in, sems):
    del after
    copy = pltpu.make_async_copy(value, value_in, sems.at[0])
    copy.start()
    step = project.shape[1] // 4
    moves = []
    for index in range(4):
        columns = pl.ds(index * step, step)
        moves.append(
            pltpu.make_async_copy(
                project.at[:, columns], project_in.at[:, columns], sems.at[index + 1]
            )
        )
        moves[index].start()
    peers, height, _ = got.shape
    heads = value.shape[0]
    chunk = ROWS * heads
    tiles = height // chunk
    stats = got[:, tiles * chunk :, :].astype(F32)
    lane = lax.broadcasted_iota(jnp.int32, (peers, ROWS, LANES), 2)
    first = lane - ROWS * lax.broadcasted_iota(jnp.int32, (peers, ROWS, LANES), 1)
    tops, totals = [], []
    for head in range(heads):
        row = jnp.broadcast_to(stats[:, head : head + 1, :], (peers, ROWS, LANES))
        tops.append(
            jnp.sum(jnp.where((first >= 0) & (first < 3), row, 0.0), axis=2, keepdims=True)
        )
        totals.append(
            jnp.sum(jnp.where((first >= 3) & (first < 6), row, 0.0), axis=2, keepdims=True)
        )
    top = jnp.concatenate(tops, axis=1)
    total = jnp.concatenate(totals, axis=1)
    peak = jnp.max(top, axis=0, keepdims=True)
    share = total * jnp.exp(top - peak)
    denominator = jnp.sum(share, axis=0)
    columns = []
    for tile in range(tiles):
        piece = got[:, tile * chunk : (tile + 1) * chunk, :].astype(F32)
        columns.append(jnp.sum(piece * share, axis=0) / denominator)
    merged = jnp.concatenate(columns, axis=1)
    values = []
    copy.wait()
    for head in range(heads):
        rows = merged[ROWS * head : ROWS * (head + 1)].astype(BF16)
        values.append(jnp.dot(rows, value_in[head], preferred_element_type=F32))
    head_values = jnp.concatenate(values, axis=1).astype(BF16)
    for index, move in enumerate(moves):
        here = slice(index * step, (index + 1) * step)
        move.wait()
        out[:, here] = jnp.dot(head_values, project_in[:, here], preferred_element_type=F32)


def merge(after, got, value, project):
    depth, width = project.shape
    return pl.pallas_call(
        merge_kernel,
        out_shape=jax.ShapeDtypeStruct((ROWS, width), F32),
        in_specs=[ANY, VMEM] + [HBM] * 2,
        out_specs=VMEM,
        scratch_shapes=[
            pltpu.VMEM(value.shape, BF16),
            pltpu.VMEM(project.shape, BF16),
            pltpu.SemaphoreType.DMA((5,)),
        ],
        compiler_params=params(16),
        cost_estimate=pl.CostEstimate(
            flops=2 * ROWS * depth * width, bytes_accessed=4 * 2**20, transcendentals=0
        ),
        name="merge",
    )(after, got, *pinned(value, project))


def finish_kernel(attended, mix, back_0, back_1, back_2, back_3, keep, send):
    peers, _, span = keep.shape
    core = lax.axis_index("c")
    back = jnp.concatenate(
        [ref[...].astype(F32) for ref in (back_0, back_1, back_2, back_3)], axis=0
    ).astype(BF16)
    mixing = mix[...][:, : 4 * CAP]
    high = mixing.astype(BF16)
    low = (mixing - high.astype(F32)).astype(BF16)
    step = 16 * span
    for parity in range(2):

        @pl.when(core == parity)
        def _():
            outs = (keep, send) if parity == 0 else (send, keep)
            for start in range(0, 2 * peers * span, step):
                here = slice(start, start + step)
                routed = jnp.dot(high, back[:, here], preferred_element_type=F32) + jnp.dot(
                    low, back[:, here], preferred_element_type=F32
                )
                both = jnp.concatenate([attended[:, here], routed], axis=0)
                for inner in range(16):
                    piece = both[:, inner * span : (inner + 1) * span]
                    outs[inner % 2][(start // span + inner) // 2] = piece.astype(BF16)


def finish(attended, mix, back, peers):
    rows, width = attended.shape
    shape = (peers, 2 * rows, width // (2 * peers))
    return pl.pallas_call(
        finish_kernel,
        out_shape=[jax.ShapeDtypeStruct(shape, BF16)] * 2,
        in_specs=[VMEM] * 6,
        out_specs=[VMEM] * 2,
        compiler_params=params(16),
        name="finish",
    )(attended, mix, *back)


def pair_kernel(keep, taken, out):
    out[...] = (keep[...].astype(F32) + taken[...].astype(F32)).astype(BF16)


def pair(keep, taken):
    return pl.pallas_call(
        pair_kernel,
        out_shape=jax.ShapeDtypeStruct(taken.shape, BF16),
        in_specs=[VMEM] * 2,
        out_specs=VMEM,
        compiler_params=params(8),
        name="pair",
    )(keep, taken)


def shards(
    query_lat,
    query_rope,
    cache_lat,
    cache_rope,
    lengths,
    w_value,
    w_out,
    moe_tokens,
    expert_ids,
    route_weights,
    w_gate,
    w_up,
    w_down,
):
    plane = ("y", "z")
    group_count = lax.axis_size("x")
    peers = lax.axis_size(plane)
    requests = cache_lat.shape[0]
    span = moe_tokens.shape[1]
    swap = [(0, 1), (1, 0)]

    def along_x(value, shift):
        return lax.ppermute(
            value, "x", [(i, (i + shift) % group_count) for i in range(group_count)]
        )

    column, depth = lax.axis_size("y"), lax.axis_size("z")
    sent = payload(query_lat, query_rope, moe_tokens, depth)
    near_query = lax.all_to_all(sent, "z", 0, 0, tiled=True)
    query = [near_query] + [
        lax.ppermute(near_query, "y", [(i, (i + d) % column) for i in range(column)])
        for d in range(1, column)
    ]
    rope_far = lax.ppermute(cache_rope, "c", swap)
    lat_far = lax.ppermute(cache_lat, "c", swap)
    scale = (w_value.shape[2] + query_rope.shape[2]) ** (-0.5)
    part, *send, mix = attention(
        lengths,
        query,
        cache_lat,
        lat_far,
        cache_rope,
        rope_far,
        expert_ids,
        route_weights,
        scale,
        span,
        w_gate.shape[1],
    )
    got = lax.all_to_all(part, plane, 0, 0, tiled=True)

    near = [send[0]] + [along_x(send[d], d) for d in range(1, group_count)]
    gate, up, down = fetch(part, w_gate, w_up, w_down)
    own = stack(gate, *near)
    far = lax.ppermute(own, "c", swap)
    routed = experts(own, far, gate, up, down)
    back = [routed[0]] + [along_x(routed[d], -d) for d in range(1, group_count)]

    attended = merge(routed[0], got, w_value, w_out)
    keep, give = finish(attended, mix, back, peers)
    terms = pair(keep, lax.ppermute(give, "c", swap))
    arrived = lax.all_to_all(terms, plane, 0, 0, tiled=True)
    summed = jnp.sum(arrived.astype(F32), axis=0).astype(BF16)
    return (summed[:requests], summed[requests:])


def solution(mesh):
    groups = mesh.shape["grp"]
    split = Mesh(mesh.devices.reshape(groups, 4, 8, 2), ("x",) + KV)
    both = ("x",) + KV
    return jax.shard_map(
        shards,
        mesh=split,
        in_specs=(
            P("x", KV, None),
            P("x", KV, None),
            P("x", KV, None),
            P("x", None, KV),
            P("x"),
            P(KV, None, None),
            P(KV, None),
            P("x", KV),
            P("x", None),
            P("x", None),
            P(None, both),
            P(None, both),
            P(both, None),
        ),
        out_specs=(P("x", KV), P("x", KV)),
        check_vma=False,
    )
```

```python
import jax
import jax.numpy as jnp
from jax import lax
from jax.experimental import pallas as pl
from jax.experimental.pallas import tpu as pltpu
from jax.sharding import Mesh
from jax.sharding import PartitionSpec as P

FF = 1024
CAP = 4
ROWS = 8
F32 = jnp.float32
BF16 = jnp.bfloat16
LANES = 128
KV = ("y", "z", "c")
VMEM = pl.BlockSpec(memory_space=pltpu.VMEM)
SMEM = pl.BlockSpec(memory_space=pltpu.SMEM)
ANY = pl.BlockSpec(memory_space=pl.ANY)
HBM = pl.BlockSpec(memory_space=pltpu.HBM)


def three_terms(value):
    high = value.astype(BF16).astype(F32)
    rest = value - high
    middle = rest.astype(BF16).astype(F32)
    return high, middle, rest - middle


def pinned(*values):
    return [pltpu.with_memory_space_constraint(value, pltpu.HBM) for value in values]


def params(mebibytes):
    return pltpu.CompilerParams(vmem_limit_bytes=mebibytes * 2**20)


def fetch_kernel(after, *refs):
    del after
    count = len(refs) // 2
    sems = refs[-1]
    copies = [
        pltpu.make_async_copy(refs[index], refs[count + index], sems.at[index])
        for index in range(count)
    ]
    for copy in copies:
        copy.start()
    for copy in copies:
        copy.wait()


def fetch(after, *values):
    moved = sum(value.size * value.dtype.itemsize for value in values)
    return pl.pallas_call(
        fetch_kernel,
        out_shape=[pltpu.VMEM(value.shape, value.dtype) for value in values],
        in_specs=[ANY] + [HBM] * len(values),
        out_specs=[VMEM] * len(values),
        scratch_shapes=[pltpu.SemaphoreType.DMA((len(values),))],
        compiler_params=params(1),
        cost_estimate=pl.CostEstimate(flops=0, bytes_accessed=moved, transcendentals=0),
        name="fetch",
    )(after, *pinned(*values))


def payload_kernel(query_lat, query_rope, tokens, out, lat_in, rope_in, tokens_in, sems):
    copies = [
        pltpu.make_async_copy(source, target, sems.at[index])
        for index, (source, target) in enumerate(
            ((query_lat, lat_in), (query_rope, rope_in), (tokens, tokens_in))
        )
    ]
    for copy in copies:
        copy.start()
    for copy in copies:
        copy.wait()
    peers = out.shape[0]
    latent, rope = query_lat.shape[2], query_rope.shape[2]
    heads = query_lat.shape[1]
    half = tokens.shape[1] // heads
    lat = lat_in[...].astype(F32)
    rot = rope_in[...].astype(F32)
    tok = tokens_in[...].astype(F32)
    spare = jnp.zeros((ROWS, out.shape[2] - latent - rope - half), F32)
    rows = []
    for head in range(heads):
        tail = jnp.concatenate(
            [rot[:, head, :], tok[:, head * half : (head + 1) * half], spare], axis=1
        )
        rows.append(jnp.concatenate([lat[:, head, :], tail], axis=1))
    chunk = jnp.concatenate(rows, axis=0).astype(BF16)
    for peer in range(peers):
        out[peer] = chunk


def payload(query_lat, query_rope, tokens, peers):
    requests, heads, latent = query_lat.shape
    return pl.pallas_call(
        payload_kernel,
        out_shape=jax.ShapeDtypeStruct((peers, heads * requests, latent + LANES), BF16),
        in_specs=[HBM] * 3,
        out_specs=VMEM,
        scratch_shapes=[
            pltpu.VMEM(query_lat.shape, BF16),
            pltpu.VMEM(query_rope.shape, BF16),
            pltpu.VMEM(tokens.shape, BF16),
            pltpu.SemaphoreType.DMA((3,)),
        ],
        compiler_params=params(20),
        name="payload",
    )(*pinned(query_lat, query_rope, tokens))


def attention_kernel(
    lengths,
    query,
    query_one,
    query_two,
    query_three,
    lat_own,
    lat_far,
    rope_own,
    rope_far,
    ids,
    route,
    out,
    send_0,
    send_1,
    send_2,
    send_3,
    mix_out,
    query_rows,
    out_rows,
    stat_rows,
    token_rows,
    lengths_in,
    lat_in,
    rope_in,
    ids_in,
    route_in,
    sems,
    *,
    scale,
    units,
):
    ring, chunk, width = query.shape
    peers = 4 * ring
    requests, positions, latent = lat_own.shape
    small = [
        pltpu.make_async_copy(lengths, lengths_in, sems.at[0]),
        pltpu.make_async_copy(ids, ids_in, sems.at[1]),
        pltpu.make_async_copy(route, route_in, sems.at[2]),
    ]
    large = [
        pltpu.make_async_copy(rope_own, rope_in, sems.at[3]),
    ] + [
        pltpu.make_async_copy(
            lat_own.at[pl.ds(half_of, requests // 2)],
            lat_in.at[pl.ds(half_of, requests // 2)],
            sems.at[4 + half_of // (requests // 2)],
        )
        for half_of in range(0, requests, requests // 2)
    ]
    for copy in small + large:
        copy.start()
    rope = rope_own.shape[1]
    tiles = latent // LANES
    heads = chunk // requests
    group, groups = lax.axis_index("x"), lax.axis_size("x")
    shard, shards_here = lax.axis_index(KV), lax.axis_size(KV)
    core = lax.axis_index("c")
    rows = peers * heads

    row = lax.axis_index("y")
    for step, source in enumerate((query, query_one, query_two, query_three)):
        begin = pl.multiple_of(lax.rem(row + 4 - step, 4) * (ring * chunk), ring * chunk)
        for tile in range(tiles + 1):
            piece = source[:, :, tile * LANES : (tile + 1) * LANES].astype(F32)
            query_rows[tile, pl.ds(begin, ring * chunk), :] = piece.reshape(ring * chunk, LANES)

    half = token_rows.shape[1] // (peers * heads)
    for peer in range(peers):
        begin = peer * chunk
        pieces = [
            query_rows[tiles, begin + requests * head : begin + requests * (head + 1), :][
                :, rope : rope + half
            ]
            for head in range(heads)
        ]
        token_rows[:, peer * heads * half : (peer + 1) * heads * half] = jnp.concatenate(
            pieces, axis=1
        )
    tokens = token_rows[...].astype(BF16)
    for copy in small:
        copy.wait()
    named = ids_in[...]
    strength = route_in[...]
    lower = (
        lax.broadcasted_iota(jnp.int32, (ROWS, ROWS), 1)
        < lax.broadcasted_iota(jnp.int32, (ROWS, ROWS), 0)
    ).astype(F32)
    slot_lane = lax.broadcasted_iota(jnp.int32, (ROWS, LANES), 1)
    placing = jnp.zeros((ROWS, LANES), F32)
    mix = jnp.zeros((ROWS, LANES), F32)
    for step in range(4):
        expert = (lax.rem(group + step, groups) * shards_here + shard) * units // FF
        hit = named == expert
        chosen = jnp.max(jnp.where(hit, 1.0, 0.0), axis=1, keepdims=True)
        weight = jnp.sum(jnp.where(hit, strength, 0.0), axis=1, keepdims=True)
        chosen_wide = jnp.broadcast_to(chosen, (ROWS, LANES))
        rank = jnp.dot(lower, chosen_wide, preferred_element_type=F32)
        picked = (rank == (slot_lane - CAP * step).astype(F32)) & (chosen_wide > 0.0)
        picked = picked & (slot_lane >= CAP * step) & (slot_lane < CAP * (step + 1))
        placing = jnp.where(picked, 1.0, placing)
        mix = jnp.where(picked, weight, mix)
    mix_out[...] = mix
    select = placing.T[: 4 * CAP, :].astype(BF16)
    chosen_rows = jnp.dot(select, tokens, preferred_element_type=F32).astype(BF16)
    for step, send in enumerate((send_0, send_1, send_2, send_3)):
        send[...] = chosen_rows[CAP * step : CAP * (step + 1)]

    lane = lax.broadcasted_iota(jnp.int32, (rows, LANES), 1)
    stats = jnp.zeros((rows, LANES), F32)
    base_own = shard * positions
    base_far = (shard + 1 - 2 * core) * positions
    place = lax.broadcasted_iota(jnp.int32, (rows, positions), 1)
    queries = []
    for request in range(requests):
        queries.append(
            jnp.concatenate(
                [
                    jnp.concatenate(
                        [
                            query_rows[
                                tile, pl.ds(requests * head + request, peers, stride=chunk), :
                            ]
                            for tile in range(tiles + 1)
                        ],
                        axis=1,
                    )
                    for head in range(heads)
                ],
                axis=0,
            ).astype(BF16)
        )

    def scores(request, lat, rot, base):
        mine = queries[request]
        score = (
            lax.dot_general(
                mine[:, :latent],
                lat[request],
                (((1,), (1,)), ((), ())),
                preferred_element_type=F32,
            )
            + jnp.dot(mine[:, latent : latent + rope], rot[request], preferred_element_type=F32)
        ) * scale
        usable = place < lengths_in[request] - base
        return jnp.where(usable, score, -1e30), usable

    for request in range(requests):
        if request == 0:
            large[0].wait()
            large[1].wait()
        if request == requests // 2:
            large[2].wait()
        parts = [
            scores(request, lat_in, rope_in, base_own),
            scores(request, lat_far, rope_far, base_far),
        ]
        top = jnp.max(jnp.maximum(parts[0][0], parts[1][0]), axis=1, keepdims=True)
        weights = [jnp.where(usable, jnp.exp(score - top), 0.0) for score, usable in parts]
        total = jnp.sum(weights[0] + weights[1], axis=1, keepdims=True)
        weighted = jnp.dot(
            weights[0].astype(BF16), lat_in[request], preferred_element_type=F32
        ) + jnp.dot(weights[1].astype(BF16), lat_far[request], preferred_element_type=F32)
        partial = weighted * (1.0 / jnp.maximum(total, 1.0))
        for index, term in enumerate(three_terms(top) + three_terms(total)):
            stats = jnp.where(lane == ROWS * request + index, term, stats)
        for head in range(heads):
            for tile in range(tiles):
                out_rows[tile, pl.ds(requests * head + request, peers, stride=chunk), :] = partial[
                    peers * head : peers * (head + 1), tile * LANES : (tile + 1) * LANES
                ]

    for tile in range(tiles):
        out[:, tile * chunk : (tile + 1) * chunk, :] = (
            out_rows[tile].reshape(peers, chunk, LANES).astype(BF16)
        )
    stat_rows[...] = jnp.zeros_like(stat_rows)
    for head in range(heads):
        stat_rows[pl.ds(head, peers, stride=ROWS), :] = stats[peers * head : peers * (head + 1)]
    out[:, tiles * chunk :, :] = stat_rows[...].reshape(peers, ROWS, LANES).astype(BF16)


def attention(lengths, query, lat_own, lat_far, rope_own, rope_far, ids, route, scale, span, units):
    peers, chunk, width = 4 * query[0].shape[0], *query[0].shape[1:]
    requests, positions, latent = lat_own.shape
    rope = rope_own.shape[1]
    tiles = latent // LANES
    lengths, lat_own, rope_own, ids, route = pinned(lengths, lat_own, rope_own, ids, route)
    return pl.pallas_call(
        lambda *refs: attention_kernel(*refs, scale=scale, units=units),
        out_shape=[jax.ShapeDtypeStruct((peers, tiles * chunk + ROWS, LANES), BF16)]
        + [jax.ShapeDtypeStruct((CAP, peers * span), BF16)] * 4
        + [jax.ShapeDtypeStruct((ROWS, LANES), F32)],
        in_specs=[HBM] + [VMEM] * 4 + [HBM, VMEM, HBM, VMEM, HBM, HBM],
        out_specs=[VMEM] * 6,
        scratch_shapes=[
            pltpu.VMEM((width // LANES, peers * chunk, LANES), F32),
            pltpu.VMEM((tiles, peers * chunk, LANES), F32),
            pltpu.VMEM((peers * ROWS, LANES), F32),
            pltpu.VMEM((requests, peers * span), F32),
            pltpu.SMEM(lengths.shape, jnp.int32),
            pltpu.VMEM(lat_own.shape, BF16),
            pltpu.VMEM(rope_own.shape, BF16),
            pltpu.VMEM(ids.shape, jnp.int32),
            pltpu.VMEM(route.shape, F32),
            pltpu.SemaphoreType.DMA((6,)),
        ],
        compiler_params=params(24),
        cost_estimate=pl.CostEstimate(
            flops=2 * peers * chunk * 2 * positions * (2 * latent + rope),
            bytes_accessed=6 * 2**20,
            transcendentals=peers * chunk * 2 * positions,
        ),
        name="attention",
    )(lengths, *query, lat_own, lat_far, rope_own, rope_far, ids, route)


def stack_kernel(after, *refs):
    del after
    out = refs[-1]
    out[...] = jnp.concatenate([ref[...].astype(F32) for ref in refs[:-1]], axis=0).astype(BF16)


def stack(after, *values):
    rows, width = values[0].shape
    return pl.pallas_call(
        stack_kernel,
        out_shape=jax.ShapeDtypeStruct((len(values) * rows, width), BF16),
        in_specs=[ANY] + [VMEM] * len(values),
        out_specs=VMEM,
        compiler_params=params(4),
        name="stack",
    )(after, *values)


def experts_kernel(own, far, gate, up, down, *outs):
    depth, units = gate.shape
    width = down.shape[1]
    span = 112
    blocks = depth // (2 * span)
    core = lax.axis_index("c")
    each = 8
    total = jnp.zeros((own.shape[0], 2 * units), F32)
    for index in range(blocks // each):
        for tokens, parity in ((own, core), (far, 1 - core)):
            columns = []
            for source in (gate, up):
                columns.append(
                    jnp.concatenate(
                        [
                            source[
                                pl.ds(
                                    pl.multiple_of(2 * span * block + span * parity, 16), span
                                ),
                                :,
                            ]
                            for block in range(each * index, each * (index + 1))
                        ],
                        axis=0,
                    )
                )
            total += jnp.dot(
                tokens[:, each * span * index : each * span * (index + 1)],
                jnp.concatenate(columns, axis=1),
                preferred_element_type=F32,
            )
    gate_proj, up_proj = total[:, :units], total[:, units:]
    hidden = (gate_proj * jax.nn.sigmoid(gate_proj) * up_proj).astype(BF16)
    step = 1024
    for start in range(0, width, step):
        here = slice(start, start + step)
        result = jnp.dot(hidden, down[:, here], preferred_element_type=F32).astype(BF16)
        for block, out in enumerate(outs):
            out[:, here] = result[CAP * block : CAP * (block + 1)]


def experts(own, far, gate, up, down):
    depth, units = gate.shape
    width = down.shape[1]
    return pl.pallas_call(
        experts_kernel,
        out_shape=[jax.ShapeDtypeStruct((CAP, width), BF16)] * 4,
        in_specs=[VMEM] * 5,
        out_specs=[VMEM] * 4,
        compiler_params=params(16),
        cost_estimate=pl.CostEstimate(
            flops=2 * 16 * 3 * depth * units, bytes_accessed=6 * 2**20, transcendentals=0
        ),
        name="experts",
    )(own, far, gate, up, down)


def merge_kernel(after, got, value, project, out, value_in, project_in, sems):
    del after
    copy = pltpu.make_async_copy(value, value_in, sems.at[0])
    copy.start()
    step = project.shape[1] // 4
    moves = []
    for index in range(4):
        columns = pl.ds(index * step, step)
        moves.append(
            pltpu.make_async_copy(
                project.at[:, columns], project_in.at[:, columns], sems.at[index + 1]
            )
        )
        moves[index].start()
    peers, height, _ = got.shape
    heads = value.shape[0]
    chunk = ROWS * heads
    tiles = height // chunk
    stats = got[:, tiles * chunk :, :].astype(F32)
    lane = lax.broadcasted_iota(jnp.int32, (peers, ROWS, LANES), 2)
    first = lane - ROWS * lax.broadcasted_iota(jnp.int32, (peers, ROWS, LANES), 1)
    tops, totals = [], []
    for head in range(heads):
        row = jnp.broadcast_to(stats[:, head : head + 1, :], (peers, ROWS, LANES))
        tops.append(
            jnp.sum(jnp.where((first >= 0) & (first < 3), row, 0.0), axis=2, keepdims=True)
        )
        totals.append(
            jnp.sum(jnp.where((first >= 3) & (first < 6), row, 0.0), axis=2, keepdims=True)
        )
    top = jnp.concatenate(tops, axis=1)
    total = jnp.concatenate(totals, axis=1)
    peak = jnp.max(top, axis=0, keepdims=True)
    share = total * jnp.exp(top - peak)
    denominator = jnp.sum(share, axis=0)
    columns = []
    for tile in range(tiles):
        piece = got[:, tile * chunk : (tile + 1) * chunk, :].astype(F32)
        columns.append(jnp.sum(piece * share, axis=0) / denominator)
    merged = jnp.concatenate(columns, axis=1)
    values = []
    copy.wait()
    for head in range(heads):
        rows = merged[ROWS * head : ROWS * (head + 1)].astype(BF16)
        values.append(jnp.dot(rows, value_in[head], preferred_element_type=F32))
    head_values = jnp.concatenate(values, axis=1).astype(BF16)
    for index, move in enumerate(moves):
        here = slice(index * step, (index + 1) * step)
        move.wait()
        out[:, here] = jnp.dot(head_values, project_in[:, here], preferred_element_type=F32)


def merge(after, got, value, project):
    depth, width = project.shape
    return pl.pallas_call(
        merge_kernel,
        out_shape=jax.ShapeDtypeStruct((ROWS, width), F32),
        in_specs=[ANY, VMEM] + [HBM] * 2,
        out_specs=VMEM,
        scratch_shapes=[
            pltpu.VMEM(value.shape, BF16),
            pltpu.VMEM(project.shape, BF16),
            pltpu.SemaphoreType.DMA((5,)),
        ],
        compiler_params=params(16),
        cost_estimate=pl.CostEstimate(
            flops=2 * ROWS * depth * width, bytes_accessed=4 * 2**20, transcendentals=0
        ),
        name="merge",
    )(after, got, *pinned(value, project))


def finish_kernel(attended, mix, back_0, back_1, back_2, back_3, keep, send):
    peers, _, span = keep.shape
    core = lax.axis_index("c")
    back = jnp.concatenate(
        [ref[...].astype(F32) for ref in (back_0, back_1, back_2, back_3)], axis=0
    ).astype(BF16)
    mixing = mix[...][:, : 4 * CAP]
    high = mixing.astype(BF16)
    low = (mixing - high.astype(F32)).astype(BF16)
    step = 16 * span
    for parity in range(2):

        @pl.when(core == parity)
        def _():
            outs = (keep, send) if parity == 0 else (send, keep)
            for start in range(0, 2 * peers * span, step):
                here = slice(start, start + step)
                routed = jnp.dot(high, back[:, here], preferred_element_type=F32) + jnp.dot(
                    low, back[:, here], preferred_element_type=F32
                )
                both = jnp.concatenate([attended[:, here], routed], axis=0)
                for inner in range(16):
                    piece = both[:, inner * span : (inner + 1) * span]
                    outs[inner % 2][(start // span + inner) // 2] = piece.astype(BF16)


def finish(attended, mix, back, peers):
    rows, width = attended.shape
    shape = (peers, 2 * rows, width // (2 * peers))
    return pl.pallas_call(
        finish_kernel,
        out_shape=[jax.ShapeDtypeStruct(shape, BF16)] * 2,
        in_specs=[VMEM] * 6,
        out_specs=[VMEM] * 2,
        compiler_params=params(16),
        name="finish",
    )(attended, mix, *back)


def pair_kernel(keep, taken, out):
    out[...] = (keep[...].astype(F32) + taken[...].astype(F32)).astype(BF16)


def pair(keep, taken):
    return pl.pallas_call(
        pair_kernel,
        out_shape=jax.ShapeDtypeStruct(taken.shape, BF16),
        in_specs=[VMEM] * 2,
        out_specs=VMEM,
        compiler_params=params(8),
        name="pair",
    )(keep, taken)


def shards(
    query_lat,
    query_rope,
    cache_lat,
    cache_rope,
    lengths,
    w_value,
    w_out,
    moe_tokens,
    expert_ids,
    route_weights,
    w_gate,
    w_up,
    w_down,
):
    plane = ("y", "z")
    group_count = lax.axis_size("x")
    peers = lax.axis_size(plane)
    requests = cache_lat.shape[0]
    span = moe_tokens.shape[1]
    swap = [(0, 1), (1, 0)]

    def along_x(value, shift):
        return lax.ppermute(
            value, "x", [(i, (i + shift) % group_count) for i in range(group_count)]
        )

    column, depth = lax.axis_size("y"), lax.axis_size("z")
    sent = payload(query_lat, query_rope, moe_tokens, depth)
    near_query = lax.all_to_all(sent, "z", 0, 0, tiled=True)
    query = [near_query] + [
        lax.ppermute(near_query, "y", [(i, (i + d) % column) for i in range(column)])
        for d in range(1, column)
    ]
    later_lat, later_rope, near_query = lax.optimization_barrier(
        (cache_lat, cache_rope, near_query)
    )
    query[0] = near_query
    lat_far = lax.ppermute(later_lat, "c", swap)
    rope_far = lax.ppermute(later_rope, "c", swap)
    scale = (w_value.shape[2] + query_rope.shape[2]) ** (-0.5)
    part, *send, mix = attention(
        lengths,
        query,
        cache_lat,
        lat_far,
        cache_rope,
        rope_far,
        expert_ids,
        route_weights,
        scale,
        span,
        w_gate.shape[1],
    )
    got = lax.all_to_all(part, plane, 0, 0, tiled=True)

    near = [send[0]] + [along_x(send[d], d) for d in range(1, group_count)]
    gate, up, down = fetch(part, w_gate, w_up, w_down)
    own = stack(gate, *near)
    far = lax.ppermute(own, "c", swap)
    routed = experts(own, far, gate, up, down)
    back = [routed[0]] + [along_x(routed[d], -d) for d in range(1, group_count)]

    attended = merge(routed[0], got, w_value, w_out)
    keep, give = finish(attended, mix, back, peers)
    terms = pair(keep, lax.ppermute(give, "c", swap))
    arrived = lax.all_to_all(terms, plane, 0, 0, tiled=True)
    summed = jnp.sum(arrived.astype(F32), axis=0).astype(BF16)
    return (summed[:requests], summed[requests:])


def solution(mesh):
    groups = mesh.shape["grp"]
    split = Mesh(mesh.devices.reshape(groups, 4, 8, 2), ("x",) + KV)
    both = ("x",) + KV
    return jax.shard_map(
        shards,
        mesh=split,
        in_specs=(
            P("x", KV, None),
            P("x", KV, None),
            P("x", KV, None),
            P("x", None, KV),
            P("x"),
            P(KV, None, None),
            P(KV, None),
            P("x", KV),
            P("x", None),
            P("x", None),
            P(None, both),
            P(None, both),
            P(both, None),
        ),
        out_specs=(P("x", KV), P("x", KV)),
        check_vma=False,
    )
```

```python
import jax
import jax.numpy as jnp
from jax import lax
from jax.experimental import pallas as pl
from jax.experimental.pallas import tpu as pltpu
from jax.sharding import Mesh
from jax.sharding import PartitionSpec as P

FF = 1024
CAP = 4
ROWS = 8
F32 = jnp.float32
BF16 = jnp.bfloat16
LANES = 128
KV = ("y", "z", "c")
VMEM = pl.BlockSpec(memory_space=pltpu.VMEM)
SMEM = pl.BlockSpec(memory_space=pltpu.SMEM)
ANY = pl.BlockSpec(memory_space=pl.ANY)
HBM = pl.BlockSpec(memory_space=pltpu.HBM)


def three_terms(value):
    high = value.astype(BF16).astype(F32)
    rest = value - high
    middle = rest.astype(BF16).astype(F32)
    return high, middle, rest - middle


def pinned(*values):
    return [pltpu.with_memory_space_constraint(value, pltpu.HBM) for value in values]


def params(mebibytes):
    return pltpu.CompilerParams(vmem_limit_bytes=mebibytes * 2**20)


def fetch_kernel(after, *refs):
    del after
    count = len(refs) // 2
    sems = refs[-1]
    copies = [
        pltpu.make_async_copy(refs[index], refs[count + index], sems.at[index])
        for index in range(count)
    ]
    for copy in copies:
        copy.start()
    for copy in copies:
        copy.wait()


def fetch(after, *values):
    moved = sum(value.size * value.dtype.itemsize for value in values)
    return pl.pallas_call(
        fetch_kernel,
        out_shape=[pltpu.VMEM(value.shape, value.dtype) for value in values],
        in_specs=[ANY] + [HBM] * len(values),
        out_specs=[VMEM] * len(values),
        scratch_shapes=[pltpu.SemaphoreType.DMA((len(values),))],
        compiler_params=params(1),
        cost_estimate=pl.CostEstimate(flops=0, bytes_accessed=moved, transcendentals=0),
        name="fetch",
    )(after, *pinned(*values))


def payload_kernel(query_lat, query_rope, tokens, out, lat_in, rope_in, tokens_in, sems):
    copies = [
        pltpu.make_async_copy(source, target, sems.at[index])
        for index, (source, target) in enumerate(
            ((query_lat, lat_in), (query_rope, rope_in), (tokens, tokens_in))
        )
    ]
    for copy in copies:
        copy.start()
    for copy in copies:
        copy.wait()
    peers = out.shape[0]
    latent, rope = query_lat.shape[2], query_rope.shape[2]
    heads = query_lat.shape[1]
    half = tokens.shape[1] // heads
    lat = lat_in[...].astype(F32)
    rot = rope_in[...].astype(F32)
    tok = tokens_in[...].astype(F32)
    spare = jnp.zeros((ROWS, out.shape[2] - latent - rope - half), F32)
    rows = []
    for head in range(heads):
        tail = jnp.concatenate(
            [rot[:, head, :], tok[:, head * half : (head + 1) * half], spare], axis=1
        )
        rows.append(jnp.concatenate([lat[:, head, :], tail], axis=1))
    chunk = jnp.concatenate(rows, axis=0).astype(BF16)
    for peer in range(peers):
        out[peer] = chunk


def payload(query_lat, query_rope, tokens, peers):
    requests, heads, latent = query_lat.shape
    return pl.pallas_call(
        payload_kernel,
        out_shape=jax.ShapeDtypeStruct((peers, heads * requests, latent + LANES), BF16),
        in_specs=[HBM] * 3,
        out_specs=VMEM,
        scratch_shapes=[
            pltpu.VMEM(query_lat.shape, BF16),
            pltpu.VMEM(query_rope.shape, BF16),
            pltpu.VMEM(tokens.shape, BF16),
            pltpu.SemaphoreType.DMA((3,)),
        ],
        compiler_params=params(20),
        name="payload",
    )(*pinned(query_lat, query_rope, tokens))


def attention_kernel(
    lengths,
    query,
    query_one,
    query_two,
    query_three,
    lat_own,
    lat_far,
    rope_own,
    rope_far,
    ids,
    route,
    out,
    send_0,
    send_1,
    send_2,
    send_3,
    mix_out,
    query_rows,
    out_rows,
    stat_rows,
    token_rows,
    lengths_in,
    lat_in,
    rope_in,
    ids_in,
    route_in,
    sems,
    *,
    scale,
    units,
):
    ring, chunk, width = query.shape
    peers = 4 * ring
    requests, positions, latent = lat_own.shape
    small = [
        pltpu.make_async_copy(lengths, lengths_in, sems.at[0]),
        pltpu.make_async_copy(ids, ids_in, sems.at[1]),
        pltpu.make_async_copy(route, route_in, sems.at[2]),
    ]
    large = [
        pltpu.make_async_copy(rope_own, rope_in, sems.at[3]),
    ] + [
        pltpu.make_async_copy(
            lat_own.at[pl.ds(half_of, requests // 2)],
            lat_in.at[pl.ds(half_of, requests // 2)],
            sems.at[4 + half_of // (requests // 2)],
        )
        for half_of in range(0, requests, requests // 2)
    ]
    for copy in small + large:
        copy.start()
    rope = rope_own.shape[1]
    tiles = latent // LANES
    heads = chunk // requests
    group, groups = lax.axis_index("x"), lax.axis_size("x")
    shard, shards_here = lax.axis_index(KV), lax.axis_size(KV)
    core = lax.axis_index("c")
    rows = peers * heads

    row = lax.axis_index("y")
    for step, source in enumerate((query, query_one, query_two, query_three)):
        begin = pl.multiple_of(lax.rem(row + 4 - step, 4) * (ring * chunk), ring * chunk)
        for tile in range(tiles + 1):
            piece = source[:, :, tile * LANES : (tile + 1) * LANES].astype(F32)
            query_rows[tile, pl.ds(begin, ring * chunk), :] = piece.reshape(ring * chunk, LANES)

    half = token_rows.shape[1] // (peers * heads)
    for peer in range(peers):
        begin = peer * chunk
        pieces = [
            query_rows[tiles, begin + requests * head : begin + requests * (head + 1), :][
                :, rope : rope + half
            ]
            for head in range(heads)
        ]
        token_rows[:, peer * heads * half : (peer + 1) * heads * half] = jnp.concatenate(
            pieces, axis=1
        )
    tokens = token_rows[...].astype(BF16)
    for copy in small:
        copy.wait()
    named = ids_in[...]
    strength = route_in[...]
    lower = (
        lax.broadcasted_iota(jnp.int32, (ROWS, ROWS), 1)
        < lax.broadcasted_iota(jnp.int32, (ROWS, ROWS), 0)
    ).astype(F32)
    slot_lane = lax.broadcasted_iota(jnp.int32, (ROWS, LANES), 1)
    placing = jnp.zeros((ROWS, LANES), F32)
    mix = jnp.zeros((ROWS, LANES), F32)
    for step in range(4):
        expert = (lax.rem(group + step, groups) * shards_here + shard) * units // FF
        hit = named == expert
        chosen = jnp.max(jnp.where(hit, 1.0, 0.0), axis=1, keepdims=True)
        weight = jnp.sum(jnp.where(hit, strength, 0.0), axis=1, keepdims=True)
        chosen_wide = jnp.broadcast_to(chosen, (ROWS, LANES))
        rank = jnp.dot(lower, chosen_wide, preferred_element_type=F32)
        picked = (rank == (slot_lane - CAP * step).astype(F32)) & (chosen_wide > 0.0)
        picked = picked & (slot_lane >= CAP * step) & (slot_lane < CAP * (step + 1))
        placing = jnp.where(picked, 1.0, placing)
        mix = jnp.where(picked, weight, mix)
    mix_out[...] = mix
    select = placing.T[: 4 * CAP, :].astype(BF16)
    chosen_rows = jnp.dot(select, tokens, preferred_element_type=F32).astype(BF16)
    for step, send in enumerate((send_0, send_1, send_2, send_3)):
        send[...] = chosen_rows[CAP * step : CAP * (step + 1)]

    lane = lax.broadcasted_iota(jnp.int32, (rows, LANES), 1)
    stats = jnp.zeros((rows, LANES), F32)
    base_own = shard * positions
    base_far = (shard + 1 - 2 * core) * positions
    place = lax.broadcasted_iota(jnp.int32, (rows, positions), 1)
    queries = []
    for request in range(requests):
        queries.append(
            jnp.concatenate(
                [
                    jnp.concatenate(
                        [
                            query_rows[
                                tile, pl.ds(requests * head + request, peers, stride=chunk), :
                            ]
                            for tile in range(tiles + 1)
                        ],
                        axis=1,
                    )
                    for head in range(heads)
                ],
                axis=0,
            ).astype(BF16)
        )

    def scores(request, lat, rot, base):
        mine = queries[request]
        score = (
            lax.dot_general(
                mine[:, :latent],
                lat[request],
                (((1,), (1,)), ((), ())),
                preferred_element_type=F32,
            )
            + jnp.dot(mine[:, latent : latent + rope], rot[request], preferred_element_type=F32)
        ) * scale
        usable = place < lengths_in[request] - base
        return jnp.where(usable, score, -1e30), usable

    for request in range(requests):
        if request == 0:
            large[0].wait()
            large[1].wait()
        if request == requests // 2:
            large[2].wait()
        parts = [
            scores(request, lat_in, rope_in, base_own),
            scores(request, lat_far, rope_far, base_far),
        ]
        top = jnp.max(jnp.maximum(parts[0][0], parts[1][0]), axis=1, keepdims=True)
        weights = [jnp.where(usable, jnp.exp(score - top), 0.0) for score, usable in parts]
        total = jnp.sum(weights[0] + weights[1], axis=1, keepdims=True)
        weighted = jnp.dot(
            weights[0].astype(BF16), lat_in[request], preferred_element_type=F32
        ) + jnp.dot(weights[1].astype(BF16), lat_far[request], preferred_element_type=F32)
        partial = weighted * (1.0 / jnp.maximum(total, 1.0))
        for index, term in enumerate(three_terms(top) + three_terms(total)):
            stats = jnp.where(lane == ROWS * request + index, term, stats)
        for head in range(heads):
            for tile in range(tiles):
                out_rows[tile, pl.ds(requests * head + request, peers, stride=chunk), :] = partial[
                    peers * head : peers * (head + 1), tile * LANES : (tile + 1) * LANES
                ]

    for tile in range(tiles):
        out[:, tile * chunk : (tile + 1) * chunk, :] = (
            out_rows[tile, : peers * chunk].reshape(peers, chunk, LANES).astype(BF16)
        )
    stat_rows[...] = jnp.zeros_like(stat_rows)
    for head in range(heads):
        stat_rows[pl.ds(head, peers, stride=ROWS), :] = stats[peers * head : peers * (head + 1)]
    out[:, tiles * chunk :, :] = stat_rows[: peers * ROWS].reshape(peers, ROWS, LANES).astype(BF16)


def attention(lengths, query, lat_own, lat_far, rope_own, rope_far, ids, route, scale, span, units):
    peers, chunk, width = 4 * query[0].shape[0], *query[0].shape[1:]
    requests, positions, latent = lat_own.shape
    rope = rope_own.shape[1]
    tiles = latent // LANES
    lengths, lat_own, rope_own, ids, route = pinned(lengths, lat_own, rope_own, ids, route)
    return pl.pallas_call(
        lambda *refs: attention_kernel(*refs, scale=scale, units=units),
        out_shape=[jax.ShapeDtypeStruct((peers, tiles * chunk + ROWS, LANES), BF16)]
        + [jax.ShapeDtypeStruct((CAP, peers * span), BF16)] * 4
        + [jax.ShapeDtypeStruct((ROWS, LANES), F32)],
        in_specs=[HBM] + [VMEM] * 4 + [HBM, VMEM, HBM, VMEM, HBM, HBM],
        out_specs=[VMEM] * 6,
        scratch_shapes=[
            pltpu.VMEM((width // LANES, (peers + 1) * chunk, LANES), F32),
            pltpu.VMEM((tiles, (peers + 1) * chunk, LANES), F32),
            pltpu.VMEM(((peers + 1) * ROWS, LANES), F32),
            pltpu.VMEM((requests, peers * span), F32),
            pltpu.SMEM(lengths.shape, jnp.int32),
            pltpu.VMEM(lat_own.shape, BF16),
            pltpu.VMEM(rope_own.shape, BF16),
            pltpu.VMEM(ids.shape, jnp.int32),
            pltpu.VMEM(route.shape, F32),
            pltpu.SemaphoreType.DMA((6,)),
        ],
        compiler_params=params(24),
        cost_estimate=pl.CostEstimate(
            flops=2 * peers * chunk * 2 * positions * (2 * latent + rope),
            bytes_accessed=6 * 2**20,
            transcendentals=peers * chunk * 2 * positions,
        ),
        name="attention",
    )(lengths, *query, lat_own, lat_far, rope_own, rope_far, ids, route)


def stack_kernel(after, *refs):
    del after
    out = refs[-1]
    out[...] = jnp.concatenate([ref[...].astype(F32) for ref in refs[:-1]], axis=0).astype(BF16)


def stack(after, *values):
    rows, width = values[0].shape
    return pl.pallas_call(
        stack_kernel,
        out_shape=jax.ShapeDtypeStruct((len(values) * rows, width), BF16),
        in_specs=[ANY] + [VMEM] * len(values),
        out_specs=VMEM,
        compiler_params=params(4),
        name="stack",
    )(after, *values)


def experts_kernel(own, far, gate, up, down, *outs):
    depth, units = gate.shape
    width = down.shape[1]
    span = 112
    blocks = depth // (2 * span)
    core = lax.axis_index("c")
    each = 8
    total = jnp.zeros((own.shape[0], 2 * units), F32)
    for index in range(blocks // each):
        for tokens, parity in ((own, core), (far, 1 - core)):
            columns = []
            for source in (gate, up):
                columns.append(
                    jnp.concatenate(
                        [
                            source[
                                pl.ds(
                                    pl.multiple_of(2 * span * block + span * parity, 16), span
                                ),
                                :,
                            ]
                            for block in range(each * index, each * (index + 1))
                        ],
                        axis=0,
                    )
                )
            total += jnp.dot(
                tokens[:, each * span * index : each * span * (index + 1)],
                jnp.concatenate(columns, axis=1),
                preferred_element_type=F32,
            )
    gate_proj, up_proj = total[:, :units], total[:, units:]
    hidden = (gate_proj * jax.nn.sigmoid(gate_proj) * up_proj).astype(BF16)
    step = 1024
    for start in range(0, width, step):
        here = slice(start, start + step)
        result = jnp.dot(hidden, down[:, here], preferred_element_type=F32).astype(BF16)
        for block, out in enumerate(outs):
            out[:, here] = result[CAP * block : CAP * (block + 1)]


def experts(own, far, gate, up, down):
    depth, units = gate.shape
    width = down.shape[1]
    return pl.pallas_call(
        experts_kernel,
        out_shape=[jax.ShapeDtypeStruct((CAP, width), BF16)] * 4,
        in_specs=[VMEM] * 5,
        out_specs=[VMEM] * 4,
        compiler_params=params(16),
        cost_estimate=pl.CostEstimate(
            flops=2 * 16 * 3 * depth * units, bytes_accessed=6 * 2**20, transcendentals=0
        ),
        name="experts",
    )(own, far, gate, up, down)


def merge_kernel(after, got, value, project, out, value_in, project_in, sems):
    del after
    copy = pltpu.make_async_copy(value, value_in, sems.at[0])
    copy.start()
    step = project.shape[1] // 4
    moves = []
    for index in range(4):
        columns = pl.ds(index * step, step)
        moves.append(
            pltpu.make_async_copy(
                project.at[:, columns], project_in.at[:, columns], sems.at[index + 1]
            )
        )
        moves[index].start()
    peers, height, _ = got.shape
    heads = value.shape[0]
    chunk = ROWS * heads
    tiles = height // chunk
    stats = got[:, tiles * chunk :, :].astype(F32)
    lane = lax.broadcasted_iota(jnp.int32, (peers, ROWS, LANES), 2)
    first = lane - ROWS * lax.broadcasted_iota(jnp.int32, (peers, ROWS, LANES), 1)
    tops, totals = [], []
    for head in range(heads):
        row = jnp.broadcast_to(stats[:, head : head + 1, :], (peers, ROWS, LANES))
        tops.append(
            jnp.sum(jnp.where((first >= 0) & (first < 3), row, 0.0), axis=2, keepdims=True)
        )
        totals.append(
            jnp.sum(jnp.where((first >= 3) & (first < 6), row, 0.0), axis=2, keepdims=True)
        )
    top = jnp.concatenate(tops, axis=1)
    total = jnp.concatenate(totals, axis=1)
    peak = jnp.max(top, axis=0, keepdims=True)
    share = total * jnp.exp(top - peak)
    denominator = jnp.sum(share, axis=0)
    columns = []
    for tile in range(tiles):
        piece = got[:, tile * chunk : (tile + 1) * chunk, :].astype(F32)
        columns.append(jnp.sum(piece * share, axis=0) / denominator)
    merged = jnp.concatenate(columns, axis=1)
    values = []
    copy.wait()
    for head in range(heads):
        rows = merged[ROWS * head : ROWS * (head + 1)].astype(BF16)
        values.append(jnp.dot(rows, value_in[head], preferred_element_type=F32))
    head_values = jnp.concatenate(values, axis=1).astype(BF16)
    for index, move in enumerate(moves):
        here = slice(index * step, (index + 1) * step)
        move.wait()
        out[:, here] = jnp.dot(head_values, project_in[:, here], preferred_element_type=F32)


def merge(after, got, value, project):
    depth, width = project.shape
    return pl.pallas_call(
        merge_kernel,
        out_shape=jax.ShapeDtypeStruct((ROWS, width), F32),
        in_specs=[ANY, VMEM] + [HBM] * 2,
        out_specs=VMEM,
        scratch_shapes=[
            pltpu.VMEM(value.shape, BF16),
            pltpu.VMEM(project.shape, BF16),
            pltpu.SemaphoreType.DMA((5,)),
        ],
        compiler_params=params(16),
        cost_estimate=pl.CostEstimate(
            flops=2 * ROWS * depth * width, bytes_accessed=4 * 2**20, transcendentals=0
        ),
        name="merge",
    )(after, got, *pinned(value, project))


def finish_kernel(attended, mix, back_0, back_1, back_2, back_3, keep, send):
    peers, _, span = keep.shape
    core = lax.axis_index("c")
    back = jnp.concatenate(
        [ref[...].astype(F32) for ref in (back_0, back_1, back_2, back_3)], axis=0
    ).astype(BF16)
    mixing = mix[...][:, : 4 * CAP]
    high = mixing.astype(BF16)
    low = (mixing - high.astype(F32)).astype(BF16)
    step = 16 * span
    for parity in range(2):

        @pl.when(core == parity)
        def _():
            outs = (keep, send) if parity == 0 else (send, keep)
            for start in range(0, 2 * peers * span, step):
                here = slice(start, start + step)
                routed = jnp.dot(high, back[:, here], preferred_element_type=F32) + jnp.dot(
                    low, back[:, here], preferred_element_type=F32
                )
                both = jnp.concatenate([attended[:, here], routed], axis=0)
                for inner in range(16):
                    piece = both[:, inner * span : (inner + 1) * span]
                    outs[inner % 2][(start // span + inner) // 2] = piece.astype(BF16)


def finish(attended, mix, back, peers):
    rows, width = attended.shape
    shape = (peers, 2 * rows, width // (2 * peers))
    return pl.pallas_call(
        finish_kernel,
        out_shape=[jax.ShapeDtypeStruct(shape, BF16)] * 2,
        in_specs=[VMEM] * 6,
        out_specs=[VMEM] * 2,
        compiler_params=params(16),
        name="finish",
    )(attended, mix, *back)


def pair_kernel(keep, taken, out):
    out[...] = (keep[...].astype(F32) + taken[...].astype(F32)).astype(BF16)


def pair(keep, taken):
    return pl.pallas_call(
        pair_kernel,
        out_shape=jax.ShapeDtypeStruct(taken.shape, BF16),
        in_specs=[VMEM] * 2,
        out_specs=VMEM,
        compiler_params=params(8),
        name="pair",
    )(keep, taken)


def shards(
    query_lat,
    query_rope,
    cache_lat,
    cache_rope,
    lengths,
    w_value,
    w_out,
    moe_tokens,
    expert_ids,
    route_weights,
    w_gate,
    w_up,
    w_down,
):
    plane = ("y", "z")
    group_count = lax.axis_size("x")
    peers = lax.axis_size(plane)
    requests = cache_lat.shape[0]
    span = moe_tokens.shape[1]
    swap = [(0, 1), (1, 0)]

    def along_x(value, shift):
        return lax.ppermute(
            value, "x", [(i, (i + shift) % group_count) for i in range(group_count)]
        )

    column, depth = lax.axis_size("y"), lax.axis_size("z")
    sent = payload(query_lat, query_rope, moe_tokens, depth)
    near_query = lax.all_to_all(sent, "z", 0, 0, tiled=True)
    query = [near_query] + [
        lax.ppermute(near_query, "y", [(i, (i + d) % column) for i in range(column)])
        for d in range(1, column)
    ]
    later_lat, later_rope, near_query = lax.optimization_barrier(
        (cache_lat, cache_rope, near_query)
    )
    query[0] = near_query
    lat_far = lax.ppermute(later_lat, "c", swap)
    rope_far = lax.ppermute(later_rope, "c", swap)
    scale = (w_value.shape[2] + query_rope.shape[2]) ** (-0.5)
    part, *send, mix = attention(
        lengths,
        query,
        cache_lat,
        lat_far,
        cache_rope,
        rope_far,
        expert_ids,
        route_weights,
        scale,
        span,
        w_gate.shape[1],
    )
    got = lax.all_to_all(part, plane, 0, 0, tiled=True)

    near = [send[0]] + [along_x(send[d], d) for d in range(1, group_count)]
    gate, up, down = fetch(part, w_gate, w_up, w_down)
    own = stack(gate, *near)
    far = lax.ppermute(own, "c", swap)
    routed = experts(own, far, gate, up, down)
    back = [routed[0]] + [along_x(routed[d], -d) for d in range(1, group_count)]

    attended = merge(routed[0], got, w_value, w_out)
    keep, give = finish(attended, mix, back, peers)
    terms = pair(keep, lax.ppermute(give, "c", swap))
    arrived = lax.all_to_all(terms, plane, 0, 0, tiled=True)
    summed = jnp.sum(arrived.astype(F32), axis=0).astype(BF16)
    return (summed[:requests], summed[requests:])


def solution(mesh):
    groups = mesh.shape["grp"]
    split = Mesh(mesh.devices.reshape(groups, 4, 8, 2), ("x",) + KV)
    both = ("x",) + KV
    return jax.shard_map(
        shards,
        mesh=split,
        in_specs=(
            P("x", KV, None),
            P("x", KV, None),
            P("x", KV, None),
            P("x", None, KV),
            P("x"),
            P(KV, None, None),
            P(KV, None),
            P("x", KV),
            P("x", None),
            P("x", None),
            P(None, both),
            P(None, both),
            P(both, None),
        ),
        out_specs=(P("x", KV), P("x", KV)),
        check_vma=False,
    )
```
